32 devices in a mesh: ia: 8 (over y, x, core), ja: 4 (over z).
Axes of the slice: x: 2, y: 2, z: 4, core: 2. Of those that a mesh axis runs over, the one named last changes fastest.
Arguments:
- amplitudes: bfloat16 [8, 8, 1600, 1600], P('ia', 'ja'), may hold values from -6 to 6
- df_slabs: bfloat16 [4, 128, 1600], P('ja'), may hold values from -0.359375 to 0.359375
- vir_irrep: int32 [25], replicated, may hold values from 0 to 1, as said below
- occ_irrep: int32 [8], replicated, may hold values from 0 to 1, as said below
- aux_irrep: int32 [4], P('ja'), may hold values from 0 to 1, as said below
Outputs:
- residual_window: float32 [8, 8, 128, 128], P('ia', 'ja')
The draws below stay inside these ranges and needn't reach their ends.
Inputs may be any that keep to these rules, and one draw needn't show every extreme that they name: `vir_irrep`: both labels occur among the tiles. `occ_irrep`: both labels occur. `aux_irrep`: both labels occur.
All inputs are finite; a program needn't handle non-finite values.
Results may differ from the reference program's by a relative error of at most 0.0029.
Values may be sent and summed in bfloat16 or wider, within the bound.
No kernel may reach another device: no remote copies, remote signals or barrier semaphores. Data moves between devices by JAX's collectives and lax.ppermute only.
A program may use at most 64 MiB of HBM per device.

```python
import jax
import jax.numpy as jnp
from jax import lax

V = 1600
TILE = 64
W = 128
NT = 25
O = 8
NAUX = 4


def parity_labels(key, count):
    first, second = jax.random.split(key)
    random_bits = jax.random.randint(first, (count,), 0, 2).astype(jnp.int32)
    order = jax.random.permutation(second, count).astype(jnp.int32)
    places = jnp.arange(count, dtype=jnp.int32)
    random_bits = jnp.where(places == order[0], jnp.int32(0), random_bits)
    random_bits = jnp.where(places == order[1], jnp.int32(1), random_bits)
    return random_bits.astype(jnp.int32)


def draw_vir_irrep(key, part):
    key = jax.random.fold_in(key, 11)
    return parity_labels(key, NT)


def draw_occ_irrep(key, part):
    key = jax.random.fold_in(key, 23)
    return parity_labels(key, O)


def draw_aux_irrep(key, part):
    key = jax.random.fold_in(key, 37)
    return parity_labels(key, NAUX)


def level_of(stream_key, dims, pieces, low, top_value):
    def one(dim, parts):
        draws = jax.random.uniform(jax.random.fold_in(jax.random.fold_in(stream_key, 6), dim), (parts,), jnp.float32, low / len(pieces), top_value / len(pieces))
        return jnp.repeat(jnp.exp(draws), dims[dim] // parts).reshape((-1,) + (1,) * (len(dims) - dim - 1))

    factor_of = one(*pieces[0])
    for cut in pieces[1:]:
        factor_of = factor_of * one(*cut)
    return factor_of


def noise(key, shape, scale, reach, cuts=(), kind=jnp.bfloat16):
    entries = scale * jax.random.normal(key, shape, jnp.float32)
    if cuts:
        entries = entries * level_of(key, shape, cuts, -0.22, 0.18)
    return jnp.clip(entries, -reach, reach).astype(kind)


def setup_inputs(seed: int = 0) -> dict:
    streams_of = jax.random.split(jax.random.key(seed), 6)
    amplitudes = noise(streams_of[0], (O, O, V, V), 1.0, 6.0, ((0, 8), (1, 4)))
    df_slabs = noise(streams_of[1], (NAUX, W, V), 0.06, 0.359375, ((0, 4),))
    vir_irrep = draw_vir_irrep(jax.random.fold_in(streams_of[5], 71), 0)
    occ_irrep = draw_occ_irrep(jax.random.fold_in(streams_of[5], 71), 0)
    aux_irrep = draw_aux_irrep(jax.random.fold_in(streams_of[5], 71), 0)
    return {"amplitudes": amplitudes, "df_slabs": df_slabs, "vir_irrep": vir_irrep, "occ_irrep": occ_irrep, "aux_irrep": aux_irrep}


def reference(amplitudes, df_slabs, vir_irrep, occ_irrep, aux_irrep):
    labels = jnp.repeat(vir_irrep, TILE, total_repeat_length=V)
    window_labels = labels[:W]
    sym_cd = jnp.bitwise_xor(labels[:, None], labels[None, :])
    bmask = jnp.bitwise_xor(window_labels[None, :, None], labels[None, None, :]) == aux_irrep[:, None, None]
    masked_b = jnp.where(bmask, df_slabs, jnp.zeros_like(df_slabs))
    flat_b = masked_b.reshape(NAUX * W, V)
    right_side = jnp.transpose(masked_b, (1, 0, 2)).reshape(W, NAUX * V)
    pair_sym = jnp.bitwise_xor(occ_irrep[:, None], occ_irrep[None, :]).reshape(O * O)
    flat_t = amplitudes.reshape(O * O, V, V)

    def one_pair(packed):
        tile, symbol = packed
        masked_t = jnp.where(sym_cd == symbol, tile, jnp.zeros_like(tile))
        half = jnp.dot(flat_b, masked_t, preferred_element_type=jnp.float32).astype(jnp.bfloat16)
        left_side = jnp.transpose(half.reshape(NAUX, W, V), (1, 0, 2)).reshape(W, NAUX * V)
        return jnp.dot(left_side, right_side.T, preferred_element_type=jnp.float32)

    ladder = lax.map(one_pair, (flat_t, pair_sym)).reshape(O, O, W, W)
    return ladder + jnp.transpose(ladder, (1, 0, 3, 2))
```

```python
import functools

import jax
import jax.numpy as jnp
from jax import lax
from jax.experimental import pallas as pl
from jax.experimental.pallas import tpu as pltpu
from jax.sharding import PartitionSpec as P

TILE = 64
ROWS = 16
SLOTS = 16
WIDTH = SLOTS * TILE
BLOCK = 256
BLOCKS = WIDTH // 128
F32 = jnp.float32
BF16 = jnp.bfloat16
VMEM_LIMIT = 32 * 1024 * 1024

smem = pl.BlockSpec(memory_space=pltpu.SMEM)
vmem = pl.BlockSpec(memory_space=pltpu.VMEM)
hbm = pl.BlockSpec(memory_space=pltpu.HBM)


def column_labels(vir_ref, tiles, columns):
    tile_of = lax.broadcasted_iota(jnp.int32, (1, columns), 1) // TILE
    labels = jnp.zeros((1, columns), jnp.int32)
    for tile in range(tiles):
        labels = jnp.where(tile_of == tile, vir_ref[tile], labels)
    return labels


def row_labels(vir_ref, first_row, rows, window):
    row = first_row + lax.broadcasted_iota(jnp.int32, (rows, 1), 0)
    labels = jnp.zeros((rows, 1), jnp.int32)
    for tile in range(window // TILE):
        labels = jnp.where(row // TILE == tile, vir_ref[tile], labels)
    return labels


def masked(block, rows_label, columns_label, aux):
    return jnp.where((rows_label ^ columns_label) == aux, block, jnp.zeros_like(block))


def piece_kernel(pieces, vir_hbm, aux_ref, slab_hbm, own_ref, piece_ref, vir_ref, slab_ref, sem):
    copies = [
        pltpu.make_async_copy(slab_hbm, slab_ref, sem.at[0]),
        pltpu.make_async_copy(vir_hbm, vir_ref, sem.at[1]),
    ]
    for copy in copies:
        copy.start()
    for copy in copies:
        copy.wait()
    count, columns, window = slab_ref.shape
    first = pl.multiple_of(lax.rem(lax.axis_index("ia"), pieces) * ROWS, ROWS)
    labels = column_labels(vir_ref, vir_ref.shape[0], columns)
    rows = row_labels(vir_ref, 0, window, window)
    for aux in range(count):
        own_ref[aux * window : (aux + 1) * window, :] = masked(slab_ref[aux].T, rows, labels, aux_ref[aux])
        piece_ref[aux * ROWS : (aux + 1) * ROWS, :] = own_ref[pl.ds(aux * window + first, ROWS), :]


def join_kernel(*refs):
    out_ref = refs[-1]
    at = 0
    for ref in refs[:-1]:
        out_ref[at : at + ref.shape[0], :] = ref[...]
        at += ref.shape[0]


def chunks(columns):
    step = 512
    starts = list(range(0, columns, step))
    if len(starts) > 1 and columns - starts[-1] < 128:
        starts.pop()
    return list(zip(starts, starts[1:] + [columns]))


def add_ladder(tile_ref, pair, slabs, ladder):
    columns = slabs.shape[1]
    window = ladder.shape[0]
    for lo, hi in chunks(columns):
        half = jnp.dot(slabs[...], tile_ref[0, pair, :, lo:hi], preferred_element_type=F32).astype(BF16)
        for start in range(0, slabs.shape[0], window):
            ladder = ladder + lax.dot_general(
                half[start : start + window],
                slabs[start : start + window, lo:hi],
                (((1,), (1,)), ((), ())),
                preferred_element_type=F32,
            )
    return ladder


def own_kernel(own_ref, t_ref, tile_ref, ladder_ref, sem):
    window = ladder_ref.shape[1]
    copies = []
    for pair in range(t_ref.shape[1]):
        copies.append(pltpu.make_async_copy(t_ref.at[0, pair], tile_ref.at[0, pair], sem.at[pair]))
        copies[-1].start()
    for pair in range(t_ref.shape[1]):
        copies[pair].wait()
        ladder_ref[pair] = add_ladder(tile_ref, pair, own_ref, jnp.zeros((window, window), F32))


def rest_kernel(pieces, others, vir_ref, occ_ref, ladder_ref, tile_ref, *refs):
    piece_refs = refs[:pieces]
    out_ref = refs[pieces]
    pairs = tile_ref.shape[1]
    send_refs = refs[pieces + 1 : pieces + 1 + pairs]
    slabs = refs[-1]
    window = out_ref.shape[1]
    row = lax.axis_index("ia")
    column = lax.axis_index("ja") * pairs
    mine = lax.rem(row, pieces)
    for m in range(pieces):
        first = pl.multiple_of((mine ^ m) * ROWS, ROWS)
        for slab in range(others):
            slabs[pl.ds(slab * window + first, ROWS), :] = piece_refs[m][slab * ROWS : (slab + 1) * ROWS, :]
    left = row_labels(vir_ref, 0, window, window)
    right = column_labels(vir_ref, window // TILE, window)
    for pair in range(pairs):
        ladder = add_ladder(tile_ref, pair, slabs, ladder_ref[pair])
        keep = (left ^ right) == (occ_ref[row] ^ occ_ref[column + pair])
        out_ref[pair] = jnp.where(keep, ladder, jnp.zeros_like(ladder))
    for step in range(pairs):
        block = out_ref[lax.rem(row + step, pairs)]
        send_refs[step][...] = block.T.astype(BF16)


def places_of(vir_ref):
    places = []
    ones = jnp.int32(0)
    for tile in range(vir_ref.shape[0]):
        label = vir_ref[tile]
        places.append((label, jnp.where(label == 1, ones, tile - ones)))
        ones = ones + label
    return places, (vir_ref.shape[0] - ones, ones)


def tile_rows(place):
    return pl.ds(pl.multiple_of(place * TILE, TILE), TILE)


def compact_rows(slab, places, numbers, label, sorted_ref):
    tiles = len(places)
    for tile, (of, place) in enumerate(places):
        sorted_ref[of, tile_rows(place), :] = slab[tile * TILE : (tile + 1) * TILE, :]
    number = jnp.where(label == 1, numbers[1], numbers[0])
    block = sorted_ref[label, :WIDTH, :].T
    column = lax.broadcasted_iota(jnp.int32, (16, WIDTH), 1)
    mark = jnp.where((column == WIDTH - 1) & (number * 2 < tiles), 1.0, 0.0).astype(BF16)
    keep = column < number * TILE
    rows = block.shape[0]
    return jnp.concatenate(
        [jnp.where(keep, block[r : r + 16], mark) for r in range(0, rows, 16)], axis=0
    )


def compact_kernel(vir_hbm, aux_ref, slab_hbm, piece_ref, vir_ref, slab_ref, sorted_ref, turned_ref, sem):
    copies = [
        pltpu.make_async_copy(slab_hbm, slab_ref, sem.at[0]),
        pltpu.make_async_copy(vir_hbm, vir_ref, sem.at[1]),
    ]
    for copy in copies:
        copy.start()
    copies[1].wait()
    places, numbers = places_of(vir_ref)
    core = lax.rem(lax.axis_index("ia"), 2)
    copies[0].wait()
    for aux in range(slab_ref.shape[0]):
        label = aux_ref[aux] ^ vir_ref[core]
        turned_ref[...] = compact_rows(slab_ref[aux], places, numbers, label, sorted_ref)
        for q in range(BLOCKS):
            piece_ref[aux, q] = turned_ref[tile_rows(core), q * 128 : (q + 1) * 128]


def sort_kernel(
    vir_ref, occ_ref, aux_ref, after_ref, slab_hbm, t_hbm, own_ref, out_ref, stage_ref,
    slab_ref, rows_ref, lists_ref, slab_sem, sem,
):
    del after_ref
    pairs = t_hbm.shape[1]
    columns = t_hbm.shape[3]
    tiles = vir_ref.shape[0]
    row = lax.axis_index("ia")
    column = lax.axis_index("ja") * pairs
    full = columns // 128
    moves = [pltpu.make_async_copy(t_hbm.at[0, pair], stage_ref.at[pair], sem.at[pair]) for pair in range(pairs)]
    for move in moves:
        move.start()
    own_copy = pltpu.make_async_copy(slab_hbm, slab_ref, slab_sem)
    own_copy.start()
    places, numbers = places_of(vir_ref)
    for label in range(2):
        for place in range(SLOTS):
            lists_ref[label, place] = -1
    for tile, (label, place) in enumerate(places):
        lists_ref[label, place] = tile
    own_copy.wait()
    count, _, window = slab_ref.shape
    for aux in range(count):
        for chunk in range(2):
            label = aux_ref[aux] ^ vir_ref[chunk]
            block = compact_rows(slab_ref[aux], places, numbers, label, rows_ref)
            for q in range(BLOCKS):
                own_ref[aux, q, chunk * TILE : (chunk + 1) * TILE, :] = block[
                    chunk * TILE : (chunk + 1) * TILE, q * 128 : (q + 1) * 128
                ]
    half = [slice(0, TILE), slice(TILE, 128)]

    for pair in range(pairs):
        moves[pair].wait()
        symbol = occ_ref[row] ^ occ_ref[column + pair]

        def block(at, carry):
            label = at // BLOCKS
            q = lax.rem(at, BLOCKS)
            known = [
                jnp.clip(lists_ref[label ^ symbol, 2 * q + upper], 0, 2 * full - 1) for upper in range(2)
            ]
            spots = [pl.ds(pl.multiple_of((k // 2) * 128, 128), 128) for k in known]
            sides = [lax.rem(k, 2) for k in known]
            for left in range(2):
                for right in range(2):

                    @pl.when((sides[0] == left) & (sides[1] == right))
                    def _(left=left, right=right):
                        for place in range(SLOTS):
                            rows = tile_rows(jnp.maximum(lists_ref[label, place], 0))
                            low, high = [stage_ref[pair, rows, spot] for spot in spots]
                            out_ref[2 * pair + label, q, place * TILE : (place + 1) * TILE, :] = (
                                jnp.concatenate([low[:, half[left]], high[:, half[right]]], axis=1)
                            )

            return carry

        lax.fori_loop(0, 2 * BLOCKS, block, 0)
        empty = jnp.zeros((TILE, TILE), BF16)
        if columns % 128:
            last = vir_ref[tiles - 1]
            end = jnp.where(last == 1, numbers[1], numbers[0]) - 1
            label = last ^ symbol
            q = jnp.minimum(end // 2, BLOCKS - 1)
            for upper in range(2):

                @pl.when((lax.rem(end, 2) == upper) & (end < SLOTS))
                def _(upper=upper):
                    for place in range(SLOTS):
                        rows = tile_rows(jnp.maximum(lists_ref[label, place], 0))
                        value = stage_ref[pair, rows, full * 128 :]
                        at = (2 * pair + label, q, slice(place * TILE, (place + 1) * TILE), slice(None))
                        both = [value, empty] if upper == 0 else [out_ref[at][:, :TILE], value]
                        out_ref[at] = jnp.concatenate(both, axis=1)

        for label in range(2):
            number = jnp.where((label ^ symbol) == 1, numbers[1], numbers[0])

            def clear_block(q, carry):
                out_ref[2 * pair + label, q] = jnp.zeros((WIDTH, 128), BF16)
                return carry

            lax.fori_loop((number + 1) // 2, BLOCKS, clear_block, 0)

            @pl.when((lax.rem(number, 2) == 1) & (number < SLOTS))
            def _():
                q = number // 2
                for place in range(SLOTS):
                    rows = slice(place * TILE, (place + 1) * TILE)
                    value = out_ref[2 * pair + label, q, rows, :]
                    out_ref[2 * pair + label, q, rows, :] = jnp.concatenate([value[:, :TILE], empty], axis=1)

        for label in range(2):

            def clear(place, carry):
                for q in range(BLOCKS):
                    out_ref[2 * pair + label, q, tile_rows(place), :] = jnp.zeros((TILE, 128), BF16)
                return carry

            lax.fori_loop(numbers[label], SLOTS, clear, 0)


def product_kernel(arrived, vir_ref, occ_ref, aux_ref, own_ref, sorted_ref, stage_ref, *refs):
    del stage_ref
    mine_refs, their_refs = refs[:arrived], refs[arrived : 2 * arrived]
    out_ref = refs[2 * arrived]
    pairs, window, _ = out_ref.shape
    send_refs = refs[2 * arrived + 1 : 2 * arrived + 1 + pairs]
    slabs_ref, half_ref, place_ref = refs[-3:]
    count = own_ref.shape[0]
    total = count * (arrived + 1)
    tiles = vir_ref.shape[0]
    row = lax.axis_index("ia")
    column = lax.axis_index("ja") * pairs
    core = lax.rem(row, 2)
    ones = jnp.int32(0)
    for tile in range(tiles):
        ones = ones + vir_ref[tile]
    smaller = jnp.where(ones * 2 < tiles, 1, 0)

    auxes = [aux_ref[aux] for aux in range(count)]
    for ref in mine_refs:
        for aux in range(count):
            mark = ref[aux, BLOCKS - 1, :16, :].astype(F32)
            marked = jnp.max(mark) > 0.5
            label = jnp.where(marked, smaller, 1 - smaller)
            auxes.append(label ^ vir_ref[core])
    places = [[jnp.int32(0)] * 2 for _ in range(total)]
    rows_of = [jnp.int32(0), jnp.int32(0)]
    labels = [[aux ^ vir_ref[chunk] for chunk in range(2)] for aux in auxes]
    for slab in range(total):
        for chunk in range(2):
            label = labels[slab][chunk]
            places[slab][chunk] = jnp.where(label == 1, rows_of[1], rows_of[0])
            rows_of = [rows_of[0] + (1 - label) * TILE, rows_of[1] + label * TILE]
    first_blocks = (rows_of[0] + (BLOCK - 1)) // BLOCK
    blocks = first_blocks + (rows_of[1] + (BLOCK - 1)) // BLOCK
    for slab in range(total):
        for chunk in range(2):
            place_ref[slab, chunk] = places[slab][chunk] + labels[slab][chunk] * first_blocks * BLOCK

    def at(slab, chunk):
        return pl.ds(pl.multiple_of(place_ref[slab, chunk], TILE), TILE)

    for aux in range(count):
        for chunk in range(2):
            for q in range(BLOCKS):
                slabs_ref[at(aux, chunk), q * 128 : (q + 1) * 128] = own_ref[
                    aux, q, chunk * TILE : (chunk + 1) * TILE, :
                ]
    for m in range(arrived):
        for aux in range(count):
            slab = (m + 1) * count + aux
            for q in range(BLOCKS):
                slabs_ref[at(slab, core), q * 128 : (q + 1) * 128] = mine_refs[m][aux, q]
                slabs_ref[at(slab, 1 - core), q * 128 : (q + 1) * 128] = their_refs[m][aux, q]

    left = row_labels(vir_ref, 0, window, window)
    right = column_labels(vir_ref, window // TILE, window)

    def one_pair(pair, carry):
        symbol = occ_ref[row] ^ occ_ref[column + pair]
        out_ref[pair] = jnp.zeros((window, window), F32)

        @pl.when((vir_ref[0] != vir_ref[1]) | (symbol == 0))
        def _():
            def first(block, inner):
                label = jnp.where(block < first_blocks, 0, 1)
                rows = pl.ds(pl.multiple_of(block * BLOCK, BLOCK), BLOCK)
                for lo in range(0, WIDTH, 512):
                    half_ref[rows, lo : lo + 512] = jnp.dot(
                        slabs_ref[rows, :],
                        jnp.concatenate(
                            [sorted_ref[2 * pair + label, (lo + at) // 128] for at in range(0, 512, 128)], axis=1
                        ),
                        preferred_element_type=F32,
                    ).astype(BF16)
                return inner

            lax.fori_loop(0, blocks, first, 0)
            ladder = jnp.zeros((window, window), F32)
            for slab in range(total):
                halves = jnp.concatenate([half_ref[at(slab, 0), :], half_ref[at(slab, 1), :]], axis=0)
                others = jnp.concatenate([slabs_ref[at(slab, 0), :], slabs_ref[at(slab, 1), :]], axis=0)
                ladder = ladder + lax.dot_general(
                    halves, others, (((1,), (1,)), ((), ())), preferred_element_type=F32
                )
            out_ref[pair] = jnp.where((left ^ right) == symbol, ladder, jnp.zeros_like(ladder))

        return carry

    lax.fori_loop(0, pairs, one_pair, 0)
    for step in range(pairs):
        block = out_ref[lax.rem(row + step, pairs)]
        send_refs[step][...] = block.T.astype(BF16)


def add_kernel(ladder_ref, *refs):
    out_ref = refs[-1]
    pairs = ladder_ref.shape[0]
    row = lax.axis_index("ia")
    for step in range(pairs):
        slot = lax.rem(row + (pairs - step), pairs)
        out_ref[0, slot] = ladder_ref[slot] + refs[step][...].astype(F32)


def in_hbm(array):
    return pltpu.with_memory_space_constraint(array, pltpu.HBM)


def params(**kwargs):
    return pltpu.CompilerParams(vmem_limit_bytes=VMEM_LIMIT, **kwargs)


def solution(mesh):
    rows_of_mesh = mesh.shape["ia"]
    columns_of_mesh = mesh.shape["ja"]

    def general(amplitudes, df_slabs, vir_irrep, occ_irrep, aux_irrep):
        occ_rows, pairs, vir_count, _ = amplitudes.shape
        count, window, _ = df_slabs.shape
        assert occ_rows == 1 and rows_of_mesh == pairs * columns_of_mesh
        pieces = 1
        while pieces * 2 <= min(rows_of_mesh, window // ROWS):
            pieces *= 2
        assert pieces * ROWS == window and rows_of_mesh % pieces == 0
        others = (columns_of_mesh - 1) * count

        own, piece = pl.pallas_call(
            functools.partial(piece_kernel, pieces),
            out_shape=(
                jax.ShapeDtypeStruct((count * window, vir_count), BF16),
                jax.ShapeDtypeStruct((count * ROWS, vir_count), BF16),
            ),
            in_specs=[hbm, smem, hbm],
            out_specs=(vmem, vmem),
            scratch_shapes=[
                pltpu.SMEM(vir_irrep.shape, jnp.int32),
                pltpu.VMEM((count, vir_count, window), BF16),
                pltpu.SemaphoreType.DMA((2,)),
            ],
            compiler_params=params(),
            name="mask_slab",
        )(in_hbm(vir_irrep), aux_irrep, in_hbm(jnp.transpose(df_slabs, (0, 2, 1))))
        got = [
            lax.ppermute(piece, "ja", [(j, j ^ s) for j in range(columns_of_mesh)])
            for s in range(columns_of_mesh - 1, 0, -1)
        ]
        tile, ladder = pl.pallas_call(
            own_kernel,
            out_shape=(
                pltpu.VMEM(amplitudes.shape, BF16),
                jax.ShapeDtypeStruct((pairs, window, window), F32),
            ),
            in_specs=[vmem, hbm],
            out_specs=(vmem, vmem),
            scratch_shapes=[pltpu.SemaphoreType.DMA((pairs,))],
            compiler_params=params(),
            cost_estimate=pl.CostEstimate(
                flops=2 * pairs * count * window * vir_count * vir_count,
                bytes_accessed=pairs * vir_count * vir_count * 2,
                transcendentals=0,
            ),
            name="own_slab",
        )(own, in_hbm(amplitudes))
        got, ladder = lax.optimization_barrier((got, ladder))
        joined = pl.pallas_call(
            join_kernel,
            out_shape=jax.ShapeDtypeStruct((others * ROWS, vir_count), BF16),
            in_specs=[vmem] * len(got),
            out_specs=vmem,
            compiler_params=params(),
            name="join_pieces",
        )(*got)
        held = {0: joined}
        for m in range(2, pieces, 2):
            held[m] = lax.ppermute(joined, "ia", [(i, i ^ m) for i in range(rows_of_mesh)])
        for m in range(0, pieces, 2):
            held[m + 1] = lax.ppermute(held[m], "ia", [(i, i ^ 1) for i in range(rows_of_mesh)])

        out = pl.pallas_call(
            functools.partial(rest_kernel, pieces, others),
            out_shape=(jax.ShapeDtypeStruct((pairs, window, window), F32),)
            + (jax.ShapeDtypeStruct((window, window), BF16),) * pairs,
            in_specs=[smem, smem, vmem, vmem] + [vmem] * pieces,
            out_specs=(vmem,) * (pairs + 1),
            scratch_shapes=[pltpu.VMEM((others * window, vir_count), BF16)],
            compiler_params=params(),
            cost_estimate=pl.CostEstimate(
                flops=2 * pairs * others * window * vir_count * vir_count,
                bytes_accessed=others * window * vir_count * 2,
                transcendentals=0,
            ),
            name="other_slabs",
        )(vir_irrep, occ_irrep, ladder, pltpu.with_memory_space_constraint(tile, pltpu.VMEM), *[held[m] for m in range(pieces)])
        return tuple(out)

    def start_compact(amplitudes, df_slabs, vir_irrep, occ_irrep, aux_irrep):
        _, pairs, vir_count, _ = amplitudes.shape
        count, window, _ = df_slabs.shape
        tiles = vir_irrep.shape[0]
        slab = in_hbm(jnp.transpose(df_slabs, (0, 2, 1)))
        piece = pl.pallas_call(
            compact_kernel,
            out_shape=jax.ShapeDtypeStruct((count, BLOCKS, TILE, 128), BF16),
            in_specs=[hbm, smem, hbm],
            out_specs=vmem,
            scratch_shapes=[
                pltpu.SMEM(vir_irrep.shape, jnp.int32),
                pltpu.VMEM((count, vir_count, window), BF16),
                pltpu.VMEM((2, vir_count, window), BF16),
                pltpu.VMEM((window, WIDTH), BF16),
                pltpu.SemaphoreType.DMA((2,)),
            ],
            compiler_params=params(),
            name="compact_piece",
        )(in_hbm(vir_irrep), aux_irrep, slab)
        mine = [
            lax.ppermute(piece, "ja", [(j, j ^ s) for j in range(columns_of_mesh)])
            for s in range(columns_of_mesh - 1, 0, -1)
        ]
        own, tile, stage = pl.pallas_call(
            sort_kernel,
            out_shape=(
                jax.ShapeDtypeStruct((count, BLOCKS, window, 128), BF16),
                pltpu.VMEM((2 * pairs, BLOCKS, WIDTH, 128), BF16),
                pltpu.VMEM((pairs, vir_count, vir_count), BF16),
            ),
            in_specs=[smem, smem, smem, pl.BlockSpec(memory_space=pl.ANY), hbm, hbm],
            out_specs=(vmem, vmem, vmem),
            scratch_shapes=[
                pltpu.VMEM((count, vir_count, window), BF16),
                pltpu.VMEM((2, vir_count, window), BF16),
                pltpu.SMEM((2, tiles), jnp.int32),
                pltpu.SemaphoreType.DMA,
                pltpu.SemaphoreType.DMA((pairs,)),
            ],
            compiler_params=params(),
            cost_estimate=pl.CostEstimate(
                flops=pairs * 2 * WIDTH * WIDTH * 8,
                bytes_accessed=pairs * vir_count * vir_count * 2,
                transcendentals=0,
            ),
            name="sort_amplitudes",
        )(vir_irrep, occ_irrep, aux_irrep, piece, slab, in_hbm(amplitudes))
        return mine, own, tile, stage

    def end_compact(mine, own, tile, stage, amplitudes, df_slabs, vir_irrep, occ_irrep, aux_irrep):
        _, pairs, _, _ = amplitudes.shape
        count, window, _ = df_slabs.shape
        total = count * columns_of_mesh
        rows = (total * window // BLOCK + 1) * BLOCK
        theirs = [lax.ppermute(p, "ia", [(i, i ^ 1) for i in range(rows_of_mesh)]) for p in mine]
        return pl.pallas_call(
            functools.partial(product_kernel, len(mine)),
            out_shape=(jax.ShapeDtypeStruct((pairs, window, window), F32),)
            + (jax.ShapeDtypeStruct((window, window), BF16),) * pairs,
            in_specs=[smem, smem, smem, vmem, vmem, pl.BlockSpec(memory_space=pl.ANY)] + [vmem] * (2 * len(mine)),
            out_specs=(vmem,) * (pairs + 1),
            scratch_shapes=[
                pltpu.VMEM((rows, WIDTH), BF16),
                pltpu.VMEM((rows, WIDTH), BF16),
                pltpu.SMEM((total, 2), jnp.int32),
            ],
            compiler_params=params(),
            cost_estimate=pl.CostEstimate(
                flops=2 * pairs * total * window * WIDTH * WIDTH,
                bytes_accessed=total * window * WIDTH * 2,
                transcendentals=0,
            ),
            name="products",
        )(
            vir_irrep, occ_irrep, aux_irrep, own,
            pltpu.with_memory_space_constraint(tile, pltpu.VMEM),
            pltpu.with_memory_space_constraint(stage, pltpu.VMEM),
            *mine, *theirs,
        )

    def finish(ladder, *sends):
        pairs, window, _ = ladder.shape
        received = []
        for step in range(pairs):
            moves = []
            for i in range(rows_of_mesh):
                for j in range(columns_of_mesh):
                    target = (j * pairs + (i + step) % pairs) * columns_of_mesh + i // pairs
                    moves.append((i * columns_of_mesh + j, target))
            received.append(lax.ppermute(sends[step], ("ia", "ja"), moves))
        return ladder, received

    def add(ladder, received):
        pairs, window, _ = ladder.shape
        return pl.pallas_call(
            add_kernel,
            out_shape=jax.ShapeDtypeStruct((1, pairs, window, window), F32),
            in_specs=[vmem] * (pairs + 1),
            out_specs=vmem,
            compiler_params=params(),
            name="add_transposed",
        )(ladder, *received)

    def local(amplitudes, df_slabs, vir_irrep, occ_irrep, aux_irrep):
        window = df_slabs.shape[1]
        operands = (amplitudes, df_slabs, vir_irrep, occ_irrep, aux_irrep)
        if window != 2 * TILE or rows_of_mesh % 2:
            return add(*finish(*general(*operands)))
        mine, own, tile, stage = start_compact(*operands)
        ones = jnp.sum(vir_irrep)
        fits = jnp.maximum(ones, vir_irrep.shape[0] - ones) <= SLOTS
        mine, own = lax.optimization_barrier((mine, own))
        ladder, received = finish(*end_compact(mine, own, tile, stage, *operands))
        return lax.cond(
            fits, lambda: add(ladder, received), lambda: add(*finish(*general(*operands)))
        )

    return jax.shard_map(
        local,
        mesh=mesh,
        in_specs=(P("ia", "ja", None, None), P("ja", None, None), P(), P(), P("ja")),
        out_specs=P("ia", "ja", None, None),
        check_vma=False,
    )
```

```python
import functools

import jax
import jax.numpy as jnp
from jax import lax
from jax.experimental import pallas as pl
from jax.experimental.pallas import tpu as pltpu
from jax.sharding import PartitionSpec as P

TILE = 64
ROWS = 16
SLOTS = 16
WIDTH = SLOTS * TILE
BLOCK = 256
BLOCKS = WIDTH // 128
F32 = jnp.float32
BF16 = jnp.bfloat16
VMEM_LIMIT = 32 * 1024 * 1024

smem = pl.BlockSpec(memory_space=pltpu.SMEM)
vmem = pl.BlockSpec(memory_space=pltpu.VMEM)
hbm = pl.BlockSpec(memory_space=pltpu.HBM)


def column_labels(vir_ref, tiles, columns):
    tile_of = lax.broadcasted_iota(jnp.int32, (1, columns), 1) // TILE
    labels = jnp.zeros((1, columns), jnp.int32)
    for tile in range(tiles):
        labels = jnp.where(tile_of == tile, vir_ref[tile], labels)
    return labels


def row_labels(vir_ref, first_row, rows, window):
    row = first_row + lax.broadcasted_iota(jnp.int32, (rows, 1), 0)
    labels = jnp.zeros((rows, 1), jnp.int32)
    for tile in range(window // TILE):
        labels = jnp.where(row // TILE == tile, vir_ref[tile], labels)
    return labels


def masked(block, rows_label, columns_label, aux):
    return jnp.where((rows_label ^ columns_label) == aux, block, jnp.zeros_like(block))


def piece_kernel(pieces, vir_hbm, aux_ref, slab_hbm, own_ref, piece_ref, vir_ref, slab_ref, sem):
    copies = [
        pltpu.make_async_copy(slab_hbm, slab_ref, sem.at[0]),
        pltpu.make_async_copy(vir_hbm, vir_ref, sem.at[1]),
    ]
    for copy in copies:
        copy.start()
    for copy in copies:
        copy.wait()
    count, columns, window = slab_ref.shape
    first = pl.multiple_of(lax.rem(lax.axis_index("ia"), pieces) * ROWS, ROWS)
    labels = column_labels(vir_ref, vir_ref.shape[0], columns)
    rows = row_labels(vir_ref, 0, window, window)
    for aux in range(count):
        own_ref[aux * window : (aux + 1) * window, :] = masked(slab_ref[aux].T, rows, labels, aux_ref[aux])
        piece_ref[aux * ROWS : (aux + 1) * ROWS, :] = own_ref[pl.ds(aux * window + first, ROWS), :]


def join_kernel(*refs):
    out_ref = refs[-1]
    at = 0
    for ref in refs[:-1]:
        out_ref[at : at + ref.shape[0], :] = ref[...]
        at += ref.shape[0]


def chunks(columns):
    step = 512
    starts = list(range(0, columns, step))
    if len(starts) > 1 and columns - starts[-1] < 128:
        starts.pop()
    return list(zip(starts, starts[1:] + [columns]))


def add_ladder(tile_ref, pair, slabs, ladder):
    columns = slabs.shape[1]
    window = ladder.shape[0]
    for lo, hi in chunks(columns):
        half = jnp.dot(slabs[...], tile_ref[0, pair, :, lo:hi], preferred_element_type=F32).astype(BF16)
        for start in range(0, slabs.shape[0], window):
            ladder = ladder + lax.dot_general(
                half[start : start + window],
                slabs[start : start + window, lo:hi],
                (((1,), (1,)), ((), ())),
                preferred_element_type=F32,
            )
    return ladder


def own_kernel(own_ref, t_ref, tile_ref, ladder_ref, sem):
    window = ladder_ref.shape[1]
    copies = []
    for pair in range(t_ref.shape[1]):
        copies.append(pltpu.make_async_copy(t_ref.at[0, pair], tile_ref.at[0, pair], sem.at[pair]))
        copies[-1].start()
    for pair in range(t_ref.shape[1]):
        copies[pair].wait()
        ladder_ref[pair] = add_ladder(tile_ref, pair, own_ref, jnp.zeros((window, window), F32))


def rest_kernel(pieces, others, vir_ref, occ_ref, ladder_ref, tile_ref, *refs):
    piece_refs = refs[:pieces]
    out_ref = refs[pieces]
    pairs = tile_ref.shape[1]
    send_ref = refs[pieces + 1]
    slabs = refs[-1]
    window = out_ref.shape[1]
    row = lax.axis_index("ia")
    column = lax.axis_index("ja") * pairs
    mine = lax.rem(row, pieces)
    for m in range(pieces):
        first = pl.multiple_of((mine ^ m) * ROWS, ROWS)
        for slab in range(others):
            slabs[pl.ds(slab * window + first, ROWS), :] = piece_refs[m][slab * ROWS : (slab + 1) * ROWS, :]
    left = row_labels(vir_ref, 0, window, window)
    right = column_labels(vir_ref, window // TILE, window)
    for pair in range(pairs):
        ladder = add_ladder(tile_ref, pair, slabs, ladder_ref[pair])
        keep = (left ^ right) == (occ_ref[row] ^ occ_ref[column + pair])
        out_ref[pair] = jnp.where(keep, ladder, jnp.zeros_like(ladder))
    for step in range(pairs):
        block = out_ref[lax.rem(row + step, pairs)]
        send_ref[step] = block.T.astype(BF16)


def places_of(vir_ref):
    places = []
    ones = jnp.int32(0)
    for tile in range(vir_ref.shape[0]):
        label = vir_ref[tile]
        places.append((label, jnp.where(label == 1, ones, tile - ones)))
        ones = ones + label
    return places, (vir_ref.shape[0] - ones, ones)


def tile_rows(place):
    return pl.ds(pl.multiple_of(place * TILE, TILE), TILE)


def compact_rows(slab, places, numbers, label, sorted_ref):
    tiles = len(places)
    for tile, (of, place) in enumerate(places):
        sorted_ref[of, tile_rows(place), :] = slab[tile * TILE : (tile + 1) * TILE, :]
    number = jnp.where(label == 1, numbers[1], numbers[0])
    block = sorted_ref[label, :WIDTH, :].T
    column = lax.broadcasted_iota(jnp.int32, (16, WIDTH), 1)
    mark = jnp.where((column == WIDTH - 1) & (number * 2 < tiles), 1.0, 0.0).astype(BF16)
    keep = column < number * TILE
    rows = block.shape[0]
    return jnp.concatenate(
        [jnp.where(keep, block[r : r + 16], mark) for r in range(0, rows, 16)], axis=0
    )


def compact_kernel(vir_hbm, aux_ref, slab_hbm, piece_ref, vir_ref, slab_ref, sorted_ref, turned_ref, sem):
    copies = [
        pltpu.make_async_copy(slab_hbm, slab_ref, sem.at[0]),
        pltpu.make_async_copy(vir_hbm, vir_ref, sem.at[1]),
    ]
    for copy in copies:
        copy.start()
    copies[1].wait()
    places, numbers = places_of(vir_ref)
    core = lax.rem(lax.axis_index("ia"), 2)
    copies[0].wait()
    for aux in range(slab_ref.shape[0]):
        label = aux_ref[aux] ^ vir_ref[core]
        turned_ref[...] = compact_rows(slab_ref[aux], places, numbers, label, sorted_ref)
        for q in range(BLOCKS):
            piece_ref[aux, q] = turned_ref[tile_rows(core), q * 128 : (q + 1) * 128]


def sort_kernel(
    vir_ref, occ_ref, aux_ref, after_ref, slab_hbm, t_hbm, own_ref, out_ref, stage_ref,
    slab_ref, rows_ref, lists_ref, slab_sem, sem,
):
    del after_ref
    pairs = t_hbm.shape[1]
    columns = t_hbm.shape[3]
    tiles = vir_ref.shape[0]
    row = lax.axis_index("ia")
    column = lax.axis_index("ja") * pairs
    full = columns // 128
    moves = [pltpu.make_async_copy(t_hbm.at[0, pair], stage_ref.at[pair], sem.at[pair]) for pair in range(pairs)]
    for move in moves:
        move.start()
    own_copy = pltpu.make_async_copy(slab_hbm, slab_ref, slab_sem)
    own_copy.start()
    places, numbers = places_of(vir_ref)
    for label in range(2):
        for place in range(SLOTS):
            lists_ref[label, place] = -1
    for tile, (label, place) in enumerate(places):
        lists_ref[label, place] = tile
    own_copy.wait()
    count, _, window = slab_ref.shape
    for aux in range(count):
        for chunk in range(2):
            label = aux_ref[aux] ^ vir_ref[chunk]
            block = compact_rows(slab_ref[aux], places, numbers, label, rows_ref)
            for q in range(BLOCKS):
                own_ref[aux, q, chunk * TILE : (chunk + 1) * TILE, :] = block[
                    chunk * TILE : (chunk + 1) * TILE, q * 128 : (q + 1) * 128
                ]
    half = [slice(0, TILE), slice(TILE, 128)]

    for pair in range(pairs):
        moves[pair].wait()
        symbol = occ_ref[row] ^ occ_ref[column + pair]

        def block(at, carry):
            label = at // BLOCKS
            q = lax.rem(at, BLOCKS)
            known = [
                jnp.clip(lists_ref[label ^ symbol, 2 * q + upper], 0, 2 * full - 1) for upper in range(2)
            ]
            spots = [pl.ds(pl.multiple_of((k // 2) * 128, 128), 128) for k in known]
            sides = [lax.rem(k, 2) for k in known]
            for left in range(2):
                for right in range(2):

                    @pl.when((sides[0] == left) & (sides[1] == right))
                    def _(left=left, right=right):
                        for group in range(0, SLOTS, 4):
                            joined = []
                            for place in range(group, group + 4):
                                rows = tile_rows(jnp.maximum(lists_ref[label, place], 0))
                                low, high = [stage_ref[pair, rows, spot] for spot in spots]
                                joined.append(
                                    jnp.concatenate([low[:, half[left]], high[:, half[right]]], axis=1)
                                )
                            out_ref[2 * pair + label, q, group * TILE : (group + 4) * TILE, :] = (
                                jnp.concatenate(joined, axis=0)
                            )

            return carry

        lax.fori_loop(0, 2 * BLOCKS, block, 0)
        empty = jnp.zeros((TILE, TILE), BF16)
        if columns % 128:
            last = vir_ref[tiles - 1]
            end = jnp.where(last == 1, numbers[1], numbers[0]) - 1
            label = last ^ symbol
            q = jnp.minimum(end // 2, BLOCKS - 1)
            for upper in range(2):

                @pl.when((lax.rem(end, 2) == upper) & (end < SLOTS))
                def _(upper=upper):
                    for place in range(SLOTS):
                        rows = tile_rows(jnp.maximum(lists_ref[label, place], 0))
                        value = stage_ref[pair, rows, full * 128 :]
                        at = (2 * pair + label, q, slice(place * TILE, (place + 1) * TILE), slice(None))
                        both = [value, empty] if upper == 0 else [out_ref[at][:, :TILE], value]
                        out_ref[at] = jnp.concatenate(both, axis=1)

        for label in range(2):
            number = jnp.where((label ^ symbol) == 1, numbers[1], numbers[0])

            def clear_block(q, carry):
                out_ref[2 * pair + label, q] = jnp.zeros((WIDTH, 128), BF16)
                return carry

            lax.fori_loop((number + 1) // 2, BLOCKS, clear_block, 0)

            @pl.when((lax.rem(number, 2) == 1) & (number < SLOTS))
            def _():
                q = number // 2
                for place in range(SLOTS):
                    rows = slice(place * TILE, (place + 1) * TILE)
                    value = out_ref[2 * pair + label, q, rows, :]
                    out_ref[2 * pair + label, q, rows, :] = jnp.concatenate([value[:, :TILE], empty], axis=1)

        for label in range(2):

            def clear(place, carry):
                for q in range(BLOCKS):
                    out_ref[2 * pair + label, q, tile_rows(place), :] = jnp.zeros((TILE, 128), BF16)
                return carry

            lax.fori_loop(numbers[label], SLOTS, clear, 0)


def product_kernel(arrived, vir_ref, occ_ref, aux_ref, own_ref, sorted_ref, stage_ref, *refs):
    del stage_ref
    mine_refs, their_refs = refs[:arrived], refs[arrived : 2 * arrived]
    out_ref = refs[2 * arrived]
    pairs, window, _ = out_ref.shape
    send_ref = refs[2 * arrived + 1]
    slabs_ref, half_ref, place_ref = refs[-3:]
    count = own_ref.shape[0]
    total = count * (arrived + 1)
    tiles = vir_ref.shape[0]
    row = lax.axis_index("ia")
    column = lax.axis_index("ja") * pairs
    core = lax.rem(row, 2)
    ones = jnp.int32(0)
    for tile in range(tiles):
        ones = ones + vir_ref[tile]
    smaller = jnp.where(ones * 2 < tiles, 1, 0)

    auxes = [aux_ref[aux] for aux in range(count)]
    for ref in mine_refs:
        for aux in range(count):
            mark = ref[aux, BLOCKS - 1, :16, :].astype(F32)
            marked = jnp.max(mark) > 0.5
            label = jnp.where(marked, smaller, 1 - smaller)
            auxes.append(label ^ vir_ref[core])
    places = [[jnp.int32(0)] * 2 for _ in range(total)]
    rows_of = [jnp.int32(0), jnp.int32(0)]
    labels = [[aux ^ vir_ref[chunk] for chunk in range(2)] for aux in auxes]
    for slab in range(total):
        for chunk in range(2):
            label = labels[slab][chunk]
            places[slab][chunk] = jnp.where(label == 1, rows_of[1], rows_of[0])
            rows_of = [rows_of[0] + (1 - label) * TILE, rows_of[1] + label * TILE]
    first_blocks = (rows_of[0] + (BLOCK - 1)) // BLOCK
    blocks = first_blocks + (rows_of[1] + (BLOCK - 1)) // BLOCK
    for slab in range(total):
        for chunk in range(2):
            place_ref[slab, chunk] = places[slab][chunk] + labels[slab][chunk] * first_blocks * BLOCK

    def at(slab, chunk):
        return pl.ds(pl.multiple_of(place_ref[slab, chunk], TILE), TILE)

    for aux in range(count):
        for chunk in range(2):
            for q in range(BLOCKS):
                slabs_ref[at(aux, chunk), q * 128 : (q + 1) * 128] = own_ref[
                    aux, q, chunk * TILE : (chunk + 1) * TILE, :
                ]
    for m in range(arrived):
        for aux in range(count):
            slab = (m + 1) * count + aux
            for q in range(BLOCKS):
                slabs_ref[at(slab, core), q * 128 : (q + 1) * 128] = mine_refs[m][aux, q]
                slabs_ref[at(slab, 1 - core), q * 128 : (q + 1) * 128] = their_refs[m][aux, q]

    left = row_labels(vir_ref, 0, window, window)
    right = column_labels(vir_ref, window // TILE, window)

    def one_pair(pair, carry):
        symbol = occ_ref[row] ^ occ_ref[column + pair]
        out_ref[pair] = jnp.zeros((window, window), F32)

        @pl.when((vir_ref[0] != vir_ref[1]) | (symbol == 0))
        def _():
            def first(block, inner):
                label = jnp.where(block < first_blocks, 0, 1)
                rows = pl.ds(pl.multiple_of(block * BLOCK, BLOCK), BLOCK)
                for lo in range(0, WIDTH, 512):
                    half_ref[rows, lo : lo + 512] = jnp.dot(
                        slabs_ref[rows, :],
                        jnp.concatenate(
                            [sorted_ref[2 * pair + label, (lo + at) // 128] for at in range(0, 512, 128)], axis=1
                        ),
                        preferred_element_type=F32,
                    ).astype(BF16)
                return inner

            lax.fori_loop(0, blocks, first, 0)
            ladder = jnp.zeros((window, window), F32)
            for slab in range(total):
                halves = jnp.concatenate([half_ref[at(slab, 0), :], half_ref[at(slab, 1), :]], axis=0)
                others = jnp.concatenate([slabs_ref[at(slab, 0), :], slabs_ref[at(slab, 1), :]], axis=0)
                ladder = ladder + lax.dot_general(
                    halves, others, (((1,), (1,)), ((), ())), preferred_element_type=F32
                )
            out_ref[pair] = jnp.where((left ^ right) == symbol, ladder, jnp.zeros_like(ladder))

        return carry

    lax.fori_loop(0, pairs, one_pair, 0)
    for step in range(pairs):
        block = out_ref[lax.rem(row + step, pairs)]
        send_ref[step] = block.T.astype(BF16)


def add_kernel(ladder_ref, *refs):
    out_ref = refs[-1]
    pairs = ladder_ref.shape[0]
    row = lax.axis_index("ia")
    for step in range(pairs):
        slot = lax.rem(row + (pairs - step), pairs)
        block = refs[step][min(step, refs[step].shape[0] - 1)]
        out_ref[0, slot] = ladder_ref[slot] + block.astype(F32)


def in_hbm(array):
    return pltpu.with_memory_space_constraint(array, pltpu.HBM)


def params(**kwargs):
    return pltpu.CompilerParams(vmem_limit_bytes=VMEM_LIMIT, **kwargs)


def solution(mesh):
    rows_of_mesh = mesh.shape["ia"]
    columns_of_mesh = mesh.shape["ja"]

    def general(amplitudes, df_slabs, vir_irrep, occ_irrep, aux_irrep):
        occ_rows, pairs, vir_count, _ = amplitudes.shape
        count, window, _ = df_slabs.shape
        assert occ_rows == 1 and rows_of_mesh == pairs * columns_of_mesh
        pieces = 1
        while pieces * 2 <= min(rows_of_mesh, window // ROWS):
            pieces *= 2
        assert pieces * ROWS == window and rows_of_mesh % pieces == 0
        others = (columns_of_mesh - 1) * count

        own, piece = pl.pallas_call(
            functools.partial(piece_kernel, pieces),
            out_shape=(
                jax.ShapeDtypeStruct((count * window, vir_count), BF16),
                jax.ShapeDtypeStruct((count * ROWS, vir_count), BF16),
            ),
            in_specs=[hbm, smem, hbm],
            out_specs=(vmem, vmem),
            scratch_shapes=[
                pltpu.SMEM(vir_irrep.shape, jnp.int32),
                pltpu.VMEM((count, vir_count, window), BF16),
                pltpu.SemaphoreType.DMA((2,)),
            ],
            compiler_params=params(),
            name="mask_slab",
        )(in_hbm(vir_irrep), aux_irrep, in_hbm(jnp.transpose(df_slabs, (0, 2, 1))))
        got = [
            lax.ppermute(piece, "ja", [(j, j ^ s) for j in range(columns_of_mesh)])
            for s in range(columns_of_mesh - 1, 0, -1)
        ]
        tile, ladder = pl.pallas_call(
            own_kernel,
            out_shape=(
                pltpu.VMEM(amplitudes.shape, BF16),
                jax.ShapeDtypeStruct((pairs, window, window), F32),
            ),
            in_specs=[vmem, hbm],
            out_specs=(vmem, vmem),
            scratch_shapes=[pltpu.SemaphoreType.DMA((pairs,))],
            compiler_params=params(),
            cost_estimate=pl.CostEstimate(
                flops=2 * pairs * count * window * vir_count * vir_count,
                bytes_accessed=pairs * vir_count * vir_count * 2,
                transcendentals=0,
            ),
            name="own_slab",
        )(own, in_hbm(amplitudes))
        got, ladder = lax.optimization_barrier((got, ladder))
        joined = pl.pallas_call(
            join_kernel,
            out_shape=jax.ShapeDtypeStruct((others * ROWS, vir_count), BF16),
            in_specs=[vmem] * len(got),
            out_specs=vmem,
            compiler_params=params(),
            name="join_pieces",
        )(*got)
        held = {0: joined}
        for m in range(2, pieces, 2):
            held[m] = lax.ppermute(joined, "ia", [(i, i ^ m) for i in range(rows_of_mesh)])
        for m in range(0, pieces, 2):
            held[m + 1] = lax.ppermute(held[m], "ia", [(i, i ^ 1) for i in range(rows_of_mesh)])

        out = pl.pallas_call(
            functools.partial(rest_kernel, pieces, others),
            out_shape=(
                jax.ShapeDtypeStruct((pairs, window, window), F32),
                jax.ShapeDtypeStruct((pairs, window, window), BF16),
            ),
            in_specs=[smem, smem, vmem, vmem] + [vmem] * pieces,
            out_specs=(vmem, vmem),
            scratch_shapes=[pltpu.VMEM((others * window, vir_count), BF16)],
            compiler_params=params(),
            cost_estimate=pl.CostEstimate(
                flops=2 * pairs * others * window * vir_count * vir_count,
                bytes_accessed=others * window * vir_count * 2,
                transcendentals=0,
            ),
            name="other_slabs",
        )(vir_irrep, occ_irrep, ladder, pltpu.with_memory_space_constraint(tile, pltpu.VMEM), *[held[m] for m in range(pieces)])
        return tuple(out)

    def start_compact(amplitudes, df_slabs, vir_irrep, occ_irrep, aux_irrep):
        _, pairs, vir_count, _ = amplitudes.shape
        count, window, _ = df_slabs.shape
        tiles = vir_irrep.shape[0]
        slab = in_hbm(jnp.transpose(df_slabs, (0, 2, 1)))
        piece = pl.pallas_call(
            compact_kernel,
            out_shape=jax.ShapeDtypeStruct((count, BLOCKS, TILE, 128), BF16),
            in_specs=[hbm, smem, hbm],
            out_specs=vmem,
            scratch_shapes=[
                pltpu.SMEM(vir_irrep.shape, jnp.int32),
                pltpu.VMEM((count, vir_count, window), BF16),
                pltpu.VMEM((2, vir_count, window), BF16),
                pltpu.VMEM((window, WIDTH), BF16),
                pltpu.SemaphoreType.DMA((2,)),
            ],
            compiler_params=params(),
            name="compact_piece",
        )(in_hbm(vir_irrep), aux_irrep, slab)
        mine = [
            lax.ppermute(piece, "ja", [(j, j ^ s) for j in range(columns_of_mesh)])
            for s in range(columns_of_mesh - 1, 0, -1)
        ]
        own, tile, stage = pl.pallas_call(
            sort_kernel,
            out_shape=(
                jax.ShapeDtypeStruct((count, BLOCKS, window, 128), BF16),
                pltpu.VMEM((2 * pairs, BLOCKS, WIDTH, 128), BF16),
                pltpu.VMEM((pairs, vir_count, vir_count), BF16),
            ),
            in_specs=[smem, smem, smem, pl.BlockSpec(memory_space=pl.ANY), hbm, hbm],
            out_specs=(vmem, vmem, vmem),
            scratch_shapes=[
                pltpu.VMEM((count, vir_count, window), BF16),
                pltpu.VMEM((2, vir_count, window), BF16),
                pltpu.SMEM((2, tiles), jnp.int32),
                pltpu.SemaphoreType.DMA,
                pltpu.SemaphoreType.DMA((pairs,)),
            ],
            compiler_params=params(),
            cost_estimate=pl.CostEstimate(
                flops=pairs * 2 * WIDTH * WIDTH * 8,
                bytes_accessed=pairs * vir_count * vir_count * 2,
                transcendentals=0,
            ),
            name="sort_amplitudes",
        )(vir_irrep, occ_irrep, aux_irrep, piece, slab, in_hbm(amplitudes))
        return mine, own, tile, stage

    def end_compact(mine, own, tile, stage, amplitudes, df_slabs, vir_irrep, occ_irrep, aux_irrep):
        _, pairs, _, _ = amplitudes.shape
        count, window, _ = df_slabs.shape
        total = count * columns_of_mesh
        rows = (total * window // BLOCK + 1) * BLOCK
        theirs = [lax.ppermute(p, "ia", [(i, i ^ 1) for i in range(rows_of_mesh)]) for p in mine]
        return pl.pallas_call(
            functools.partial(product_kernel, len(mine)),
            out_shape=(
                jax.ShapeDtypeStruct((pairs, window, window), F32),
                jax.ShapeDtypeStruct((pairs, window, window), BF16),
            ),
            in_specs=[smem, smem, smem, vmem, vmem, pl.BlockSpec(memory_space=pl.ANY)] + [vmem] * (2 * len(mine)),
            out_specs=(vmem, vmem),
            scratch_shapes=[
                pltpu.VMEM((rows, WIDTH), BF16),
                pltpu.VMEM((rows, WIDTH), BF16),
                pltpu.SMEM((total, 2), jnp.int32),
            ],
            compiler_params=params(),
            cost_estimate=pl.CostEstimate(
                flops=2 * pairs * total * window * WIDTH * WIDTH,
                bytes_accessed=total * window * WIDTH * 2,
                transcendentals=0,
            ),
            name="products",
        )(
            vir_irrep, occ_irrep, aux_irrep, own,
            pltpu.with_memory_space_constraint(tile, pltpu.VMEM),
            pltpu.with_memory_space_constraint(stage, pltpu.VMEM),
            *mine, *theirs,
        )

    def finish(ladder, sends):
        pairs = ladder.shape[0]

        def moves(step):
            return [
                (
                    i * columns_of_mesh + j,
                    (j * pairs + (i + step) % pairs) * columns_of_mesh + i // pairs,
                )
                for i in range(rows_of_mesh)
                for j in range(columns_of_mesh)
            ]

        if pairs != 2:
            return ladder, [
                lax.ppermute(sends[step : step + 1], ("ia", "ja"), moves(step)) for step in range(pairs)
            ]
        first = lax.ppermute(sends, ("ia", "ja"), moves(0))
        second = lax.ppermute(first, "ia", [(i, i ^ 1) for i in range(rows_of_mesh)])
        return ladder, [first, second]

    def add(ladder, received):
        pairs, window, _ = ladder.shape
        return pl.pallas_call(
            add_kernel,
            out_shape=jax.ShapeDtypeStruct((1, pairs, window, window), F32),
            in_specs=[vmem] * (pairs + 1),
            out_specs=vmem,
            compiler_params=params(),
            name="add_transposed",
        )(ladder, *received)

    def local(amplitudes, df_slabs, vir_irrep, occ_irrep, aux_irrep):
        window = df_slabs.shape[1]
        operands = (amplitudes, df_slabs, vir_irrep, occ_irrep, aux_irrep)
        if window != 2 * TILE or rows_of_mesh % 2:
            return add(*finish(*general(*operands)))
        mine, own, tile, stage = start_compact(*operands)
        ones = jnp.sum(vir_irrep)
        fits = jnp.maximum(ones, vir_irrep.shape[0] - ones) <= SLOTS
        mine, own = lax.optimization_barrier((mine, own))
        ladder, received = finish(*end_compact(mine, own, tile, stage, *operands))
        return lax.cond(
            fits, lambda: add(ladder, received), lambda: add(*finish(*general(*operands)))
        )

    return jax.shard_map(
        local,
        mesh=mesh,
        in_specs=(P("ia", "ja", None, None), P("ja", None, None), P(), P(), P("ja")),
        out_specs=P("ia", "ja", None, None),
        check_vma=False,
    )
```

```python
import functools

import jax
import jax.numpy as jnp
from jax import lax
from jax.experimental import pallas as pl
from jax.experimental.pallas import tpu as pltpu
from jax.sharding import PartitionSpec as P

TILE = 64
ROWS = 16
SLOTS = 16
WIDTH = SLOTS * TILE
BLOCK = 256
BLOCKS = WIDTH // 128
GROUP = 4
F32 = jnp.float32
BF16 = jnp.bfloat16
VMEM_LIMIT = 32 * 1024 * 1024

smem = pl.BlockSpec(memory_space=pltpu.SMEM)
vmem = pl.BlockSpec(memory_space=pltpu.VMEM)
hbm = pl.BlockSpec(memory_space=pltpu.HBM)


def column_labels(vir_ref, tiles, columns):
    tile_of = lax.broadcasted_iota(jnp.int32, (1, columns), 1) // TILE
    labels = jnp.zeros((1, columns), jnp.int32)
    for tile in range(tiles):
        labels = jnp.where(tile_of == tile, vir_ref[tile], labels)
    return labels


def row_labels(vir_ref, first_row, rows, window):
    row = first_row + lax.broadcasted_iota(jnp.int32, (rows, 1), 0)
    labels = jnp.zeros((rows, 1), jnp.int32)
    for tile in range(window // TILE):
        labels = jnp.where(row // TILE == tile, vir_ref[tile], labels)
    return labels


def masked(block, rows_label, columns_label, aux):
    return jnp.where((rows_label ^ columns_label) == aux, block, jnp.zeros_like(block))


def piece_kernel(pieces, vir_hbm, aux_ref, slab_hbm, own_ref, piece_ref, vir_ref, slab_ref, sem):
    copies = [
        pltpu.make_async_copy(slab_hbm, slab_ref, sem.at[0]),
        pltpu.make_async_copy(vir_hbm, vir_ref, sem.at[1]),
    ]
    for copy in copies:
        copy.start()
    for copy in copies:
        copy.wait()
    count, columns, window = slab_ref.shape
    first = pl.multiple_of(lax.rem(lax.axis_index("ia"), pieces) * ROWS, ROWS)
    labels = column_labels(vir_ref, vir_ref.shape[0], columns)
    rows = row_labels(vir_ref, 0, window, window)
    for aux in range(count):
        own_ref[aux * window : (aux + 1) * window, :] = masked(slab_ref[aux].T, rows, labels, aux_ref[aux])
        piece_ref[aux * ROWS : (aux + 1) * ROWS, :] = own_ref[pl.ds(aux * window + first, ROWS), :]


def join_kernel(*refs):
    out_ref = refs[-1]
    at = 0
    for ref in refs[:-1]:
        out_ref[at : at + ref.shape[0], :] = ref[...]
        at += ref.shape[0]


def chunks(columns):
    step = 512
    starts = list(range(0, columns, step))
    if len(starts) > 1 and columns - starts[-1] < 128:
        starts.pop()
    return list(zip(starts, starts[1:] + [columns]))


def add_ladder(tile_ref, pair, slabs, ladder):
    columns = slabs.shape[1]
    window = ladder.shape[0]
    for lo, hi in chunks(columns):
        half = jnp.dot(slabs[...], tile_ref[0, pair, :, lo:hi], preferred_element_type=F32).astype(BF16)
        for start in range(0, slabs.shape[0], window):
            ladder = ladder + lax.dot_general(
                half[start : start + window],
                slabs[start : start + window, lo:hi],
                (((1,), (1,)), ((), ())),
                preferred_element_type=F32,
            )
    return ladder


def own_kernel(own_ref, t_ref, tile_ref, ladder_ref, sem):
    window = ladder_ref.shape[1]
    copies = []
    for pair in range(t_ref.shape[1]):
        copies.append(pltpu.make_async_copy(t_ref.at[0, pair], tile_ref.at[0, pair], sem.at[pair]))
        copies[-1].start()
    for pair in range(t_ref.shape[1]):
        copies[pair].wait()
        ladder_ref[pair] = add_ladder(tile_ref, pair, own_ref, jnp.zeros((window, window), F32))


def rest_kernel(pieces, others, vir_ref, occ_ref, ladder_ref, tile_ref, *refs):
    piece_refs = refs[:pieces]
    out_ref = refs[pieces]
    pairs = tile_ref.shape[1]
    send_ref = refs[pieces + 1]
    slabs = refs[-1]
    window = out_ref.shape[1]
    row = lax.axis_index("ia")
    column = lax.axis_index("ja") * pairs
    mine = lax.rem(row, pieces)
    for m in range(pieces):
        first = pl.multiple_of((mine ^ m) * ROWS, ROWS)
        for slab in range(others):
            slabs[pl.ds(slab * window + first, ROWS), :] = piece_refs[m][slab * ROWS : (slab + 1) * ROWS, :]
    left = row_labels(vir_ref, 0, window, window)
    right = column_labels(vir_ref, window // TILE, window)
    for pair in range(pairs):
        ladder = add_ladder(tile_ref, pair, slabs, ladder_ref[pair])
        keep = (left ^ right) == (occ_ref[row] ^ occ_ref[column + pair])
        out_ref[pair] = jnp.where(keep, ladder, jnp.zeros_like(ladder))
    for step in range(pairs):
        block = out_ref[lax.rem(row + step, pairs)]
        send_ref[step] = block.T.astype(BF16)


def places_of(vir_ref):
    places = []
    ones = jnp.int32(0)
    for tile in range(vir_ref.shape[0]):
        label = vir_ref[tile]
        places.append((label, jnp.where(label == 1, ones, tile - ones)))
        ones = ones + label
    return places, (vir_ref.shape[0] - ones, ones)


def tile_rows(place):
    return pl.ds(pl.multiple_of(place * TILE, TILE), TILE)


def compact_rows(slab, places, numbers, label, sorted_ref):
    tiles = len(places)
    for tile, (of, place) in enumerate(places):
        sorted_ref[of, tile_rows(place), :] = slab[tile * TILE : (tile + 1) * TILE, :]
    number = jnp.where(label == 1, numbers[1], numbers[0])
    block = sorted_ref[label, :WIDTH, :].T
    column = lax.broadcasted_iota(jnp.int32, (16, WIDTH), 1)
    mark = jnp.where((column == WIDTH - 1) & (number * 2 < tiles), 1.0, 0.0).astype(BF16)
    keep = column < number * TILE
    rows = block.shape[0]
    return jnp.concatenate(
        [jnp.where(keep, block[r : r + 16], mark) for r in range(0, rows, 16)], axis=0
    )


def compact_kernel(vir_hbm, aux_ref, slab_hbm, piece_ref, fits_ref, vir_ref, slab_ref, sorted_ref, turned_ref, sem):
    copies = [
        pltpu.make_async_copy(slab_hbm, slab_ref, sem.at[0]),
        pltpu.make_async_copy(vir_hbm, vir_ref, sem.at[1]),
    ]
    for copy in copies:
        copy.start()
    copies[1].wait()
    places, numbers = places_of(vir_ref)
    fits_ref[0] = jnp.where(jnp.maximum(numbers[0], numbers[1]) <= SLOTS, 1, 0)
    core = lax.rem(lax.axis_index("ia"), 2)
    copies[0].wait()
    for aux in range(slab_ref.shape[0]):
        label = aux_ref[aux] ^ vir_ref[core]
        turned_ref[...] = compact_rows(slab_ref[aux], places, numbers, label, sorted_ref)
        for q in range(BLOCKS):
            piece_ref[aux, q] = turned_ref[tile_rows(core), q * 128 : (q + 1) * 128]


def sort_kernel(
    vir_ref, occ_ref, aux_ref, after_ref, slab_hbm, t_hbm, own_ref, out_ref, stage_ref,
    slab_ref, rows_ref, lists_ref, slab_sem, sem,
):
    del after_ref
    pairs = t_hbm.shape[1]
    columns = t_hbm.shape[3]
    tiles = vir_ref.shape[0]
    row = lax.axis_index("ia")
    column = lax.axis_index("ja") * pairs
    full = columns // 128
    moves = [pltpu.make_async_copy(t_hbm.at[0, pair], stage_ref.at[pair], sem.at[pair]) for pair in range(pairs)]
    for move in moves:
        move.start()
    own_copy = pltpu.make_async_copy(slab_hbm, slab_ref, slab_sem)
    own_copy.start()
    places, numbers = places_of(vir_ref)
    for label in range(2):
        for place in range(SLOTS):
            lists_ref[label, place] = -1
    for tile, (label, place) in enumerate(places):
        lists_ref[label, place] = tile
    own_copy.wait()
    count, _, window = slab_ref.shape
    for aux in range(count):
        for chunk in range(2):
            label = aux_ref[aux] ^ vir_ref[chunk]
            block = compact_rows(slab_ref[aux], places, numbers, label, rows_ref)
            for q in range(BLOCKS):
                own_ref[aux, q, chunk * TILE : (chunk + 1) * TILE, :] = block[
                    chunk * TILE : (chunk + 1) * TILE, q * 128 : (q + 1) * 128
                ]
    half = [slice(0, TILE), slice(TILE, 128)]
    for pair in range(pairs):
        moves[pair].wait()
        symbol = occ_ref[row] ^ occ_ref[column + pair]

        for label in range(2):
            rows_of = jnp.where(label == 1, numbers[1], numbers[0])
            columns_of = jnp.where((label ^ symbol) == 1, numbers[1], numbers[0])

            def block(q, carry, label=label, rows_of=rows_of):
                known = [
                    jnp.clip(lists_ref[label ^ symbol, 2 * q + upper], 0, 2 * full - 1) for upper in range(2)
                ]
                spots = [pl.ds(pl.multiple_of((k // 2) * 128, 128), 128) for k in known]
                sides = [lax.rem(k, 2) for k in known]

                def move(left, right, number):
                    for group in range(0, number, GROUP):
                        joined = []
                        for place in range(group, group + GROUP):
                            rows = tile_rows(jnp.maximum(lists_ref[label, place], 0))
                            low, high = [stage_ref[pair, rows, spot] for spot in spots]
                            joined.append(jnp.concatenate([low[:, half[left]], high[:, half[right]]], axis=1))
                        out_ref[2 * pair + label, q, group * TILE : (group + GROUP) * TILE, :] = (
                            jnp.concatenate(joined, axis=0)
                        )

                for left in range(2):
                    for right in range(2):
                        here = (sides[0] == left) & (sides[1] == right)
                        few = rows_of <= SLOTS - GROUP
                        pl.when(here & few)(functools.partial(move, left, right, SLOTS - GROUP))
                        pl.when(here & jnp.logical_not(few))(functools.partial(move, left, right, SLOTS))
                return carry

            lax.fori_loop(0, jnp.minimum((columns_of + 1) // 2, BLOCKS), block, 0)
        empty = jnp.zeros((TILE, TILE), BF16)
        if columns % 128:
            last = vir_ref[tiles - 1]
            end = jnp.where(last == 1, numbers[1], numbers[0]) - 1
            label = last ^ symbol
            q = jnp.minimum(end // 2, BLOCKS - 1)
            for upper in range(2):

                @pl.when((lax.rem(end, 2) == upper) & (end < SLOTS))
                def _(upper=upper):
                    for place in range(SLOTS):
                        rows = tile_rows(jnp.maximum(lists_ref[label, place], 0))
                        value = stage_ref[pair, rows, full * 128 :]
                        at = (2 * pair + label, q, slice(place * TILE, (place + 1) * TILE), slice(None))
                        both = [value, empty] if upper == 0 else [out_ref[at][:, :TILE], value]
                        out_ref[at] = jnp.concatenate(both, axis=1)

        for label in range(2):
            number = jnp.where((label ^ symbol) == 1, numbers[1], numbers[0])

            def clear_block(q, carry):
                out_ref[2 * pair + label, q] = jnp.zeros((WIDTH, 128), BF16)
                return carry

            lax.fori_loop((number + 1) // 2, BLOCKS, clear_block, 0)

            @pl.when((lax.rem(number, 2) == 1) & (number < SLOTS))
            def _():
                q = number // 2
                for place in range(SLOTS):
                    rows = slice(place * TILE, (place + 1) * TILE)
                    value = out_ref[2 * pair + label, q, rows, :]
                    out_ref[2 * pair + label, q, rows, :] = jnp.concatenate([value[:, :TILE], empty], axis=1)

        for label in range(2):

            def clear(place, carry):
                for q in range(BLOCKS):
                    out_ref[2 * pair + label, q, tile_rows(place), :] = jnp.zeros((TILE, 128), BF16)
                return carry

            lax.fori_loop(numbers[label], SLOTS, clear, 0)


def product_kernel(arrived, vir_ref, occ_ref, aux_ref, own_ref, sorted_ref, stage_ref, *refs):
    del stage_ref
    mine_refs, their_refs = refs[:arrived], refs[arrived : 2 * arrived]
    out_ref = refs[2 * arrived]
    pairs, window, _ = out_ref.shape
    send_ref = refs[2 * arrived + 1]
    slabs_ref, half_ref, place_ref = refs[-3:]
    count = own_ref.shape[0]
    total = count * (arrived + 1)
    tiles = vir_ref.shape[0]
    row = lax.axis_index("ia")
    column = lax.axis_index("ja") * pairs
    core = lax.rem(row, 2)
    ones = jnp.int32(0)
    for tile in range(tiles):
        ones = ones + vir_ref[tile]
    smaller = jnp.where(ones * 2 < tiles, 1, 0)

    auxes = [aux_ref[aux] for aux in range(count)]
    for ref in mine_refs:
        for aux in range(count):
            mark = ref[aux, BLOCKS - 1, :16, :].astype(F32)
            marked = jnp.max(mark) > 0.5
            label = jnp.where(marked, smaller, 1 - smaller)
            auxes.append(label ^ vir_ref[core])
    places = [[jnp.int32(0)] * 2 for _ in range(total)]
    rows_of = [jnp.int32(0), jnp.int32(0)]
    labels = [[aux ^ vir_ref[chunk] for chunk in range(2)] for aux in auxes]
    for slab in range(total):
        for chunk in range(2):
            label = labels[slab][chunk]
            places[slab][chunk] = jnp.where(label == 1, rows_of[1], rows_of[0])
            rows_of = [rows_of[0] + (1 - label) * TILE, rows_of[1] + label * TILE]
    first_blocks = (rows_of[0] + (BLOCK - 1)) // BLOCK
    blocks = first_blocks + (rows_of[1] + (BLOCK - 1)) // BLOCK
    for slab in range(total):
        for chunk in range(2):
            place_ref[slab, chunk] = places[slab][chunk] + labels[slab][chunk] * first_blocks * BLOCK

    def at(slab, chunk):
        return pl.ds(pl.multiple_of(place_ref[slab, chunk], TILE), TILE)

    for aux in range(count):
        for chunk in range(2):
            for q in range(BLOCKS):
                slabs_ref[at(aux, chunk), q * 128 : (q + 1) * 128] = own_ref[
                    aux, q, chunk * TILE : (chunk + 1) * TILE, :
                ]
    for m in range(arrived):
        for aux in range(count):
            slab = (m + 1) * count + aux
            for q in range(BLOCKS):
                slabs_ref[at(slab, core), q * 128 : (q + 1) * 128] = mine_refs[m][aux, q]
                slabs_ref[at(slab, 1 - core), q * 128 : (q + 1) * 128] = their_refs[m][aux, q]

    left = row_labels(vir_ref, 0, window, window)
    right = column_labels(vir_ref, window // TILE, window)

    def one_pair(pair, carry):
        symbol = occ_ref[row] ^ occ_ref[column + pair]
        out_ref[pair] = jnp.zeros((window, window), F32)

        @pl.when((vir_ref[0] != vir_ref[1]) | (symbol == 0))
        def _():
            def first(block, inner):
                label = jnp.where(block < first_blocks, 0, 1)
                rows = pl.ds(pl.multiple_of(block * BLOCK, BLOCK), BLOCK)
                for lo in range(0, WIDTH, 512):
                    half_ref[rows, lo : lo + 512] = jnp.dot(
                        slabs_ref[rows, :],
                        jnp.concatenate(
                            [sorted_ref[2 * pair + label, (lo + at) // 128] for at in range(0, 512, 128)], axis=1
                        ),
                        preferred_element_type=F32,
                    ).astype(BF16)
                return inner

            lax.fori_loop(0, blocks, first, 0)
            ladder = jnp.zeros((window, window), F32)
            for slab in range(total):
                halves = jnp.concatenate([half_ref[at(slab, 0), :], half_ref[at(slab, 1), :]], axis=0)
                others = jnp.concatenate([slabs_ref[at(slab, 0), :], slabs_ref[at(slab, 1), :]], axis=0)
                ladder = ladder + lax.dot_general(
                    halves, others, (((1,), (1,)), ((), ())), preferred_element_type=F32
                )
            out_ref[pair] = jnp.where((left ^ right) == symbol, ladder, jnp.zeros_like(ladder))

        return carry

    lax.fori_loop(0, pairs, one_pair, 0)
    for step in range(pairs):
        block = out_ref[lax.rem(row + step, pairs)]
        send_ref[step] = block.T.astype(BF16)


def add_kernel(ladder_ref, *refs):
    out_ref = refs[-1]
    pairs = ladder_ref.shape[0]
    row = lax.axis_index("ia")
    for step in range(pairs):
        slot = lax.rem(row + (pairs - step), pairs)
        block = refs[step][min(step, refs[step].shape[0] - 1)]
        out_ref[0, slot] = ladder_ref[slot] + block.astype(F32)


def in_hbm(array):
    return pltpu.with_memory_space_constraint(array, pltpu.HBM)


def params(**kwargs):
    return pltpu.CompilerParams(vmem_limit_bytes=VMEM_LIMIT, **kwargs)


def solution(mesh):
    rows_of_mesh = mesh.shape["ia"]
    columns_of_mesh = mesh.shape["ja"]

    def general(amplitudes, df_slabs, vir_irrep, occ_irrep, aux_irrep):
        occ_rows, pairs, vir_count, _ = amplitudes.shape
        count, window, _ = df_slabs.shape
        assert occ_rows == 1 and rows_of_mesh == pairs * columns_of_mesh
        pieces = 1
        while pieces * 2 <= min(rows_of_mesh, window // ROWS):
            pieces *= 2
        assert pieces * ROWS == window and rows_of_mesh % pieces == 0
        others = (columns_of_mesh - 1) * count

        own, piece = pl.pallas_call(
            functools.partial(piece_kernel, pieces),
            out_shape=(
                jax.ShapeDtypeStruct((count * window, vir_count), BF16),
                jax.ShapeDtypeStruct((count * ROWS, vir_count), BF16),
            ),
            in_specs=[hbm, smem, hbm],
            out_specs=(vmem, vmem),
            scratch_shapes=[
                pltpu.SMEM(vir_irrep.shape, jnp.int32),
                pltpu.VMEM((count, vir_count, window), BF16),
                pltpu.SemaphoreType.DMA((2,)),
            ],
            compiler_params=params(),
            name="mask_slab",
        )(in_hbm(vir_irrep), aux_irrep, in_hbm(jnp.transpose(df_slabs, (0, 2, 1))))
        got = [
            lax.ppermute(piece, "ja", [(j, j ^ s) for j in range(columns_of_mesh)])
            for s in range(columns_of_mesh - 1, 0, -1)
        ]
        tile, ladder = pl.pallas_call(
            own_kernel,
            out_shape=(
                pltpu.VMEM(amplitudes.shape, BF16),
                jax.ShapeDtypeStruct((pairs, window, window), F32),
            ),
            in_specs=[vmem, hbm],
            out_specs=(vmem, vmem),
            scratch_shapes=[pltpu.SemaphoreType.DMA((pairs,))],
            compiler_params=params(),
            cost_estimate=pl.CostEstimate(
                flops=2 * pairs * count * window * vir_count * vir_count,
                bytes_accessed=pairs * vir_count * vir_count * 2,
                transcendentals=0,
            ),
            name="own_slab",
        )(own, in_hbm(amplitudes))
        got, ladder = lax.optimization_barrier((got, ladder))
        joined = pl.pallas_call(
            join_kernel,
            out_shape=jax.ShapeDtypeStruct((others * ROWS, vir_count), BF16),
            in_specs=[vmem] * len(got),
            out_specs=vmem,
            compiler_params=params(),
            name="join_pieces",
        )(*got)
        held = {0: joined}
        for m in range(2, pieces, 2):
            held[m] = lax.ppermute(joined, "ia", [(i, i ^ m) for i in range(rows_of_mesh)])
        for m in range(0, pieces, 2):
            held[m + 1] = lax.ppermute(held[m], "ia", [(i, i ^ 1) for i in range(rows_of_mesh)])

        out = pl.pallas_call(
            functools.partial(rest_kernel, pieces, others),
            out_shape=(
                jax.ShapeDtypeStruct((pairs, window, window), F32),
                jax.ShapeDtypeStruct((pairs, window, window), BF16),
            ),
            in_specs=[smem, smem, vmem, vmem] + [vmem] * pieces,
            out_specs=(vmem, vmem),
            scratch_shapes=[pltpu.VMEM((others * window, vir_count), BF16)],
            compiler_params=params(),
            cost_estimate=pl.CostEstimate(
                flops=2 * pairs * others * window * vir_count * vir_count,
                bytes_accessed=others * window * vir_count * 2,
                transcendentals=0,
            ),
            name="other_slabs",
        )(vir_irrep, occ_irrep, ladder, pltpu.with_memory_space_constraint(tile, pltpu.VMEM), *[held[m] for m in range(pieces)])
        return tuple(out)

    def first_piece(df_slabs, vir_irrep, aux_irrep):
        count, window, vir_count = df_slabs.shape
        return pl.pallas_call(
            compact_kernel,
            out_shape=(
                jax.ShapeDtypeStruct((count, BLOCKS, TILE, 128), BF16),
                jax.ShapeDtypeStruct((1,), jnp.int32),
            ),
            in_specs=[hbm, smem, hbm],
            out_specs=(vmem, smem),
            scratch_shapes=[
                pltpu.SMEM(vir_irrep.shape, jnp.int32),
                pltpu.VMEM((count, vir_count, window), BF16),
                pltpu.VMEM((2, vir_count, window), BF16),
                pltpu.VMEM((window, WIDTH), BF16),
                pltpu.SemaphoreType.DMA((2,)),
            ],
            compiler_params=params(),
            name="compact_piece",
        )(in_hbm(vir_irrep), aux_irrep, in_hbm(jnp.transpose(df_slabs, (0, 2, 1))))

    def start_compact(piece, amplitudes, df_slabs, vir_irrep, occ_irrep, aux_irrep):
        _, pairs, vir_count, _ = amplitudes.shape
        count, window, _ = df_slabs.shape
        tiles = vir_irrep.shape[0]
        slab = in_hbm(jnp.transpose(df_slabs, (0, 2, 1)))
        mine = [
            lax.ppermute(piece, "ja", [(j, j ^ s) for j in range(columns_of_mesh)])
            for s in range(columns_of_mesh - 1, 0, -1)
        ]
        own, tile, stage = pl.pallas_call(
            sort_kernel,
            out_shape=(
                jax.ShapeDtypeStruct((count, BLOCKS, window, 128), BF16),
                pltpu.VMEM((2 * pairs, BLOCKS, WIDTH, 128), BF16),
                pltpu.VMEM((pairs, vir_count, vir_count), BF16),
            ),
            in_specs=[smem, smem, smem, pl.BlockSpec(memory_space=pl.ANY), hbm, hbm],
            out_specs=(vmem, vmem, vmem),
            scratch_shapes=[
                pltpu.VMEM((count, vir_count, window), BF16),
                pltpu.VMEM((2, vir_count, window), BF16),
                pltpu.SMEM((2, tiles), jnp.int32),
                pltpu.SemaphoreType.DMA,
                pltpu.SemaphoreType.DMA((pairs,)),
            ],
            compiler_params=params(),
            cost_estimate=pl.CostEstimate(
                flops=pairs * 2 * WIDTH * WIDTH * 8,
                bytes_accessed=pairs * vir_count * vir_count * 2,
                transcendentals=0,
            ),
            name="sort_amplitudes",
        )(vir_irrep, occ_irrep, aux_irrep, piece, slab, in_hbm(amplitudes))
        return mine, own, tile, stage

    def end_compact(mine, own, tile, stage, amplitudes, df_slabs, vir_irrep, occ_irrep, aux_irrep):
        _, pairs, _, _ = amplitudes.shape
        count, window, _ = df_slabs.shape
        total = count * columns_of_mesh
        rows = (total * window // BLOCK + 1) * BLOCK
        theirs = [lax.ppermute(p, "ia", [(i, i ^ 1) for i in range(rows_of_mesh)]) for p in mine]
        return pl.pallas_call(
            functools.partial(product_kernel, len(mine)),
            out_shape=(
                jax.ShapeDtypeStruct((pairs, window, window), F32),
                jax.ShapeDtypeStruct((pairs, window, window), BF16),
            ),
            in_specs=[smem, smem, smem, vmem, vmem, pl.BlockSpec(memory_space=pl.ANY)] + [vmem] * (2 * len(mine)),
            out_specs=(vmem, vmem),
            scratch_shapes=[
                pltpu.VMEM((rows, WIDTH), BF16),
                pltpu.VMEM((rows, WIDTH), BF16),
                pltpu.SMEM((total, 2), jnp.int32),
            ],
            compiler_params=params(),
            cost_estimate=pl.CostEstimate(
                flops=2 * pairs * total * window * WIDTH * WIDTH,
                bytes_accessed=total * window * WIDTH * 2,
                transcendentals=0,
            ),
            name="products",
        )(
            vir_irrep, occ_irrep, aux_irrep, own,
            pltpu.with_memory_space_constraint(tile, pltpu.VMEM),
            pltpu.with_memory_space_constraint(stage, pltpu.VMEM),
            *mine, *theirs,
        )

    def finish(ladder, sends):
        pairs = ladder.shape[0]

        def moves(step):
            return [
                (
                    i * columns_of_mesh + j,
                    (j * pairs + (i + step) % pairs) * columns_of_mesh + i // pairs,
                )
                for i in range(rows_of_mesh)
                for j in range(columns_of_mesh)
            ]

        if pairs != 2:
            return ladder, [
                lax.ppermute(sends[step : step + 1], ("ia", "ja"), moves(step)) for step in range(pairs)
            ]
        first = lax.ppermute(sends, ("ia", "ja"), moves(0))
        second = lax.ppermute(first, "ia", [(i, i ^ 1) for i in range(rows_of_mesh)])
        return ladder, [first, second]

    def add(ladder, received):
        pairs, window, _ = ladder.shape
        return pl.pallas_call(
            add_kernel,
            out_shape=jax.ShapeDtypeStruct((1, pairs, window, window), F32),
            in_specs=[vmem] * (pairs + 1),
            out_specs=vmem,
            compiler_params=params(),
            name="add_transposed",
        )(ladder, *received)

    def local(amplitudes, df_slabs, vir_irrep, occ_irrep, aux_irrep):
        window = df_slabs.shape[1]
        operands = (amplitudes, df_slabs, vir_irrep, occ_irrep, aux_irrep)
        if window != 2 * TILE or rows_of_mesh % 2:
            return add(*finish(*general(*operands)))
        piece, fits = first_piece(df_slabs, vir_irrep, aux_irrep)

        def compact():
            mine, own, tile, stage = start_compact(piece, *operands)
            mine, own = lax.optimization_barrier((mine, own))
            return add(*finish(*end_compact(mine, own, tile, stage, *operands)))

        return lax.cond(fits[0] == 1, compact, lambda: add(*finish(*general(*operands))))

    return jax.shard_map(
        local,
        mesh=mesh,
        in_specs=(P("ia", "ja", None, None), P("ja", None, None), P(), P(), P("ja")),
        out_specs=P("ia", "ja", None, None),
        check_vma=False,
    )
```

```python
import functools

import jax
import jax.numpy as jnp
from jax import lax
from jax.experimental import pallas as pl
from jax.experimental.pallas import tpu as pltpu
from jax.sharding import PartitionSpec as P

TILE = 64
ROWS = 16
SLOTS = 16
WIDTH = SLOTS * TILE
BLOCK = 256
BLOCKS = WIDTH // 128
GROUP = 4
F32 = jnp.float32
BF16 = jnp.bfloat16
VMEM_LIMIT = 32 * 1024 * 1024

smem = pl.BlockSpec(memory_space=pltpu.SMEM)
vmem = pl.BlockSpec(memory_space=pltpu.VMEM)
hbm = pl.BlockSpec(memory_space=pltpu.HBM)


def column_labels(vir_ref, tiles, columns):
    tile_of = lax.broadcasted_iota(jnp.int32, (1, columns), 1) // TILE
    labels = jnp.zeros((1, columns), jnp.int32)
    for tile in range(tiles):
        labels = jnp.where(tile_of == tile, vir_ref[tile], labels)
    return labels


def row_labels(vir_ref, first_row, rows, window):
    row = first_row + lax.broadcasted_iota(jnp.int32, (rows, 1), 0)
    labels = jnp.zeros((rows, 1), jnp.int32)
    for tile in range(window // TILE):
        labels = jnp.where(row // TILE == tile, vir_ref[tile], labels)
    return labels


def masked(block, rows_label, columns_label, aux):
    return jnp.where((rows_label ^ columns_label) == aux, block, jnp.zeros_like(block))


def piece_kernel(pieces, vir_hbm, aux_ref, slab_hbm, own_ref, piece_ref, vir_ref, slab_ref, sem):
    copies = [
        pltpu.make_async_copy(slab_hbm, slab_ref, sem.at[0]),
        pltpu.make_async_copy(vir_hbm, vir_ref, sem.at[1]),
    ]
    for copy in copies:
        copy.start()
    for copy in copies:
        copy.wait()
    count, columns, window = slab_ref.shape
    first = pl.multiple_of(lax.rem(lax.axis_index("ia"), pieces) * ROWS, ROWS)
    labels = column_labels(vir_ref, vir_ref.shape[0], columns)
    rows = row_labels(vir_ref, 0, window, window)
    for aux in range(count):
        own_ref[aux * window : (aux + 1) * window, :] = masked(slab_ref[aux].T, rows, labels, aux_ref[aux])
        piece_ref[aux * ROWS : (aux + 1) * ROWS, :] = own_ref[pl.ds(aux * window + first, ROWS), :]


def join_kernel(*refs):
    out_ref = refs[-1]
    at = 0
    for ref in refs[:-1]:
        out_ref[at : at + ref.shape[0], :] = ref[...]
        at += ref.shape[0]


def chunks(columns):
    step = 512
    starts = list(range(0, columns, step))
    if len(starts) > 1 and columns - starts[-1] < 128:
        starts.pop()
    return list(zip(starts, starts[1:] + [columns]))


def add_ladder(tile_ref, pair, slabs, ladder):
    columns = slabs.shape[1]
    window = ladder.shape[0]
    for lo, hi in chunks(columns):
        half = jnp.dot(slabs[...], tile_ref[0, pair, :, lo:hi], preferred_element_type=F32).astype(BF16)
        for start in range(0, slabs.shape[0], window):
            ladder = ladder + lax.dot_general(
                half[start : start + window],
                slabs[start : start + window, lo:hi],
                (((1,), (1,)), ((), ())),
                preferred_element_type=F32,
            )
    return ladder


def own_kernel(own_ref, t_ref, tile_ref, ladder_ref, sem):
    window = ladder_ref.shape[1]
    copies = []
    for pair in range(t_ref.shape[1]):
        copies.append(pltpu.make_async_copy(t_ref.at[0, pair], tile_ref.at[0, pair], sem.at[pair]))
        copies[-1].start()
    for pair in range(t_ref.shape[1]):
        copies[pair].wait()
        ladder_ref[pair] = add_ladder(tile_ref, pair, own_ref, jnp.zeros((window, window), F32))


def rest_kernel(pieces, others, vir_ref, occ_ref, ladder_ref, tile_ref, *refs):
    piece_refs = refs[:pieces]
    out_ref = refs[pieces]
    pairs = tile_ref.shape[1]
    send_ref = refs[pieces + 1]
    slabs = refs[-1]
    window = out_ref.shape[1]
    row = lax.axis_index("ia")
    column = lax.axis_index("ja") * pairs
    mine = lax.rem(row, pieces)
    for m in range(pieces):
        first = pl.multiple_of((mine ^ m) * ROWS, ROWS)
        for slab in range(others):
            slabs[pl.ds(slab * window + first, ROWS), :] = piece_refs[m][slab * ROWS : (slab + 1) * ROWS, :]
    left = row_labels(vir_ref, 0, window, window)
    right = column_labels(vir_ref, window // TILE, window)
    for pair in range(pairs):
        ladder = add_ladder(tile_ref, pair, slabs, ladder_ref[pair])
        keep = (left ^ right) == (occ_ref[row] ^ occ_ref[column + pair])
        out_ref[pair] = jnp.where(keep, ladder, jnp.zeros_like(ladder))
    for step in range(pairs):
        block = out_ref[lax.rem(row + step, pairs)]
        send_ref[step] = block.T.astype(BF16)


def places_of(vir_ref):
    places = []
    ones = jnp.int32(0)
    for tile in range(vir_ref.shape[0]):
        label = vir_ref[tile]
        places.append((label, jnp.where(label == 1, ones, tile - ones)))
        ones = ones + label
    return places, (vir_ref.shape[0] - ones, ones)


def tile_rows(place):
    return pl.ds(pl.multiple_of(place * TILE, TILE), TILE)


def compact_rows(slab, places, numbers, label, sorted_ref):
    tiles = len(places)
    for tile, (of, place) in enumerate(places):
        sorted_ref[of, tile_rows(place), :] = slab[tile * TILE : (tile + 1) * TILE, :]
    number = jnp.where(label == 1, numbers[1], numbers[0])
    block = sorted_ref[label, :WIDTH, :].T
    column = lax.broadcasted_iota(jnp.int32, (16, WIDTH), 1)
    mark = jnp.where((column == WIDTH - 1) & (number * 2 < tiles), 1.0, 0.0).astype(BF16)
    keep = column < number * TILE
    rows = block.shape[0]
    return jnp.concatenate(
        [jnp.where(keep, block[r : r + 16], mark) for r in range(0, rows, 16)], axis=0
    )


def compact_kernel(vir_hbm, aux_ref, slab_hbm, piece_ref, fits_ref, vir_ref, slab_ref, sorted_ref, turned_ref, sem):
    copies = [
        pltpu.make_async_copy(slab_hbm, slab_ref, sem.at[0]),
        pltpu.make_async_copy(vir_hbm, vir_ref, sem.at[1]),
    ]
    for copy in copies:
        copy.start()
    copies[1].wait()
    places, numbers = places_of(vir_ref)
    fits_ref[0] = jnp.where(jnp.maximum(numbers[0], numbers[1]) <= SLOTS, 1, 0)
    core = lax.rem(lax.axis_index("ia"), 2)
    copies[0].wait()
    for aux in range(slab_ref.shape[0]):
        label = aux_ref[aux] ^ vir_ref[core]
        turned_ref[...] = compact_rows(slab_ref[aux], places, numbers, label, sorted_ref)
        for q in range(BLOCKS):
            piece_ref[aux, q] = turned_ref[tile_rows(core), q * 128 : (q + 1) * 128]


def sort_kernel(
    vir_ref, occ_ref, aux_ref, after_ref, slab_hbm, t_hbm, own_ref, out_ref, stage_ref,
    slab_ref, rows_ref, lists_ref, slab_sem, sem,
):
    del after_ref
    pairs = t_hbm.shape[1]
    columns = t_hbm.shape[3]
    tiles = vir_ref.shape[0]
    row = lax.axis_index("ia")
    column = lax.axis_index("ja") * pairs
    full = columns // 128
    moves = [pltpu.make_async_copy(t_hbm.at[0, pair], stage_ref.at[pair], sem.at[pair]) for pair in range(pairs)]
    for move in moves:
        move.start()
    own_copy = pltpu.make_async_copy(slab_hbm, slab_ref, slab_sem)
    own_copy.start()
    places, numbers = places_of(vir_ref)
    for label in range(2):
        for place in range(SLOTS):
            lists_ref[label, place] = -1
    for tile, (label, place) in enumerate(places):
        lists_ref[label, place] = tile
    own_copy.wait()
    count, _, window = slab_ref.shape
    for aux in range(count):
        for chunk in range(2):
            label = aux_ref[aux] ^ vir_ref[chunk]
            block = compact_rows(slab_ref[aux], places, numbers, label, rows_ref)
            for q in range(BLOCKS):
                own_ref[aux, q, chunk * TILE : (chunk + 1) * TILE, :] = block[
                    chunk * TILE : (chunk + 1) * TILE, q * 128 : (q + 1) * 128
                ]
    lower = lax.broadcasted_iota(jnp.int32, (TILE, 128), 1) < TILE
    for pair in range(pairs):
        moves[pair].wait()
        symbol = occ_ref[row] ^ occ_ref[column + pair]

        for label in range(2):
            rows_of = jnp.where(label == 1, numbers[1], numbers[0])
            columns_of = jnp.where((label ^ symbol) == 1, numbers[1], numbers[0])

            def block(q, carry, label=label, rows_of=rows_of):
                known = [
                    jnp.clip(lists_ref[label ^ symbol, 2 * q + upper], 0, 2 * full - 1) for upper in range(2)
                ]
                spots = [pl.ds(pl.multiple_of((k // 2) * 128, 128), 128) for k in known]
                sides = [lax.rem(k, 2) for k in known]

                def move(left, right, number):
                    for group in range(0, number, GROUP):
                        joined = []
                        for place in range(group, group + GROUP):
                            rows = tile_rows(jnp.maximum(lists_ref[label, place], 0))
                            low, high = [stage_ref[pair, rows, spot] for spot in spots]
                            if left and not right:
                                value = pltpu.roll(jnp.where(lower, high, low), TILE, 1)
                            else:
                                value = jnp.where(
                                    lower,
                                    pltpu.roll(low, TILE, 1) if left else low,
                                    high if right else pltpu.roll(high, TILE, 1),
                                )
                            joined.append(value)
                        out_ref[2 * pair + label, q, group * TILE : (group + GROUP) * TILE, :] = (
                            jnp.concatenate(joined, axis=0)
                        )

                for left in range(2):
                    for right in range(2):
                        here = (sides[0] == left) & (sides[1] == right)
                        few = rows_of <= SLOTS - GROUP
                        pl.when(here & few)(functools.partial(move, left, right, SLOTS - GROUP))
                        pl.when(here & jnp.logical_not(few))(functools.partial(move, left, right, SLOTS))
                return carry

            lax.fori_loop(0, jnp.minimum((columns_of + 1) // 2, BLOCKS), block, 0)
        empty = jnp.zeros((TILE, TILE), BF16)
        if columns % 128:
            last = vir_ref[tiles - 1]
            end = jnp.where(last == 1, numbers[1], numbers[0]) - 1
            label = last ^ symbol
            q = jnp.minimum(end // 2, BLOCKS - 1)
            for upper in range(2):

                @pl.when((lax.rem(end, 2) == upper) & (end < SLOTS))
                def _(upper=upper):
                    for place in range(SLOTS):
                        rows = tile_rows(jnp.maximum(lists_ref[label, place], 0))
                        value = stage_ref[pair, rows, full * 128 :]
                        at = (2 * pair + label, q, slice(place * TILE, (place + 1) * TILE), slice(None))
                        both = [value, empty] if upper == 0 else [out_ref[at][:, :TILE], value]
                        out_ref[at] = jnp.concatenate(both, axis=1)

        for label in range(2):
            number = jnp.where((label ^ symbol) == 1, numbers[1], numbers[0])

            def clear_block(q, carry):
                out_ref[2 * pair + label, q] = jnp.zeros((WIDTH, 128), BF16)
                return carry

            lax.fori_loop((number + 1) // 2, BLOCKS, clear_block, 0)

            @pl.when((lax.rem(number, 2) == 1) & (number < SLOTS))
            def _():
                q = number // 2
                for place in range(SLOTS):
                    rows = slice(place * TILE, (place + 1) * TILE)
                    value = out_ref[2 * pair + label, q, rows, :]
                    out_ref[2 * pair + label, q, rows, :] = jnp.concatenate([value[:, :TILE], empty], axis=1)

        for label in range(2):

            def clear(place, carry):
                for q in range(BLOCKS):
                    out_ref[2 * pair + label, q, tile_rows(place), :] = jnp.zeros((TILE, 128), BF16)
                return carry

            lax.fori_loop(numbers[label], SLOTS, clear, 0)


def product_kernel(arrived, vir_ref, occ_ref, aux_ref, own_ref, sorted_ref, stage_ref, *refs):
    del stage_ref
    mine_refs, their_refs = refs[:arrived], refs[arrived : 2 * arrived]
    out_ref = refs[2 * arrived]
    pairs, window, _ = out_ref.shape
    send_ref = refs[2 * arrived + 1]
    slabs_ref, half_ref, place_ref = refs[-3:]
    count = own_ref.shape[0]
    total = count * (arrived + 1)
    tiles = vir_ref.shape[0]
    row = lax.axis_index("ia")
    column = lax.axis_index("ja") * pairs
    core = lax.rem(row, 2)
    ones = jnp.int32(0)
    for tile in range(tiles):
        ones = ones + vir_ref[tile]
    smaller = jnp.where(ones * 2 < tiles, 1, 0)

    auxes = [aux_ref[aux] for aux in range(count)]
    for ref in mine_refs:
        for aux in range(count):
            mark = ref[aux, BLOCKS - 1, :16, :].astype(F32)
            marked = jnp.max(mark) > 0.5
            label = jnp.where(marked, smaller, 1 - smaller)
            auxes.append(label ^ vir_ref[core])
    places = [[jnp.int32(0)] * 2 for _ in range(total)]
    rows_of = [jnp.int32(0), jnp.int32(0)]
    labels = [[aux ^ vir_ref[chunk] for chunk in range(2)] for aux in auxes]
    for slab in range(total):
        for chunk in range(2):
            label = labels[slab][chunk]
            places[slab][chunk] = jnp.where(label == 1, rows_of[1], rows_of[0])
            rows_of = [rows_of[0] + (1 - label) * TILE, rows_of[1] + label * TILE]
    first_blocks = (rows_of[0] + (BLOCK - 1)) // BLOCK
    blocks = first_blocks + (rows_of[1] + (BLOCK - 1)) // BLOCK
    for slab in range(total):
        for chunk in range(2):
            place_ref[slab, chunk] = places[slab][chunk] + labels[slab][chunk] * first_blocks * BLOCK

    def at(slab, chunk):
        return pl.ds(pl.multiple_of(place_ref[slab, chunk], TILE), TILE)

    for aux in range(count):
        for chunk in range(2):
            for q in range(BLOCKS):
                slabs_ref[at(aux, chunk), q * 128 : (q + 1) * 128] = own_ref[
                    aux, q, chunk * TILE : (chunk + 1) * TILE, :
                ]
    for m in range(arrived):
        for aux in range(count):
            slab = (m + 1) * count + aux
            for q in range(BLOCKS):
                slabs_ref[at(slab, core), q * 128 : (q + 1) * 128] = mine_refs[m][aux, q]
                slabs_ref[at(slab, 1 - core), q * 128 : (q + 1) * 128] = their_refs[m][aux, q]

    left = row_labels(vir_ref, 0, window, window)
    right = column_labels(vir_ref, window // TILE, window)

    def one_pair(pair, carry):
        symbol = occ_ref[row] ^ occ_ref[column + pair]
        out_ref[pair] = jnp.zeros((window, window), F32)

        @pl.when((vir_ref[0] != vir_ref[1]) | (symbol == 0))
        def _():
            def first(block, inner):
                label = jnp.where(block < first_blocks, 0, 1)
                rows = pl.ds(pl.multiple_of(block * BLOCK, BLOCK), BLOCK)
                for lo in range(0, WIDTH, 512):
                    half_ref[rows, lo : lo + 512] = jnp.dot(
                        slabs_ref[rows, :],
                        jnp.concatenate(
                            [sorted_ref[2 * pair + label, (lo + at) // 128] for at in range(0, 512, 128)], axis=1
                        ),
                        preferred_element_type=F32,
                    ).astype(BF16)
                return inner

            lax.fori_loop(0, blocks, first, 0)
            ladder = jnp.zeros((window, window), F32)
            for slab in range(total):
                halves = jnp.concatenate([half_ref[at(slab, 0), :], half_ref[at(slab, 1), :]], axis=0)
                others = jnp.concatenate([slabs_ref[at(slab, 0), :], slabs_ref[at(slab, 1), :]], axis=0)
                ladder = ladder + lax.dot_general(
                    halves, others, (((1,), (1,)), ((), ())), preferred_element_type=F32
                )
            out_ref[pair] = jnp.where((left ^ right) == symbol, ladder, jnp.zeros_like(ladder))

        return carry

    lax.fori_loop(0, pairs, one_pair, 0)
    for step in range(pairs):
        block = out_ref[lax.rem(row + step, pairs)]
        send_ref[step] = block.T.astype(BF16)


def add_kernel(ladder_ref, *refs):
    out_ref = refs[-1]
    pairs = ladder_ref.shape[0]
    row = lax.axis_index("ia")
    for step in range(pairs):
        slot = lax.rem(row + (pairs - step), pairs)
        block = refs[step][min(step, refs[step].shape[0] - 1)]
        out_ref[0, slot] = ladder_ref[slot] + block.astype(F32)


def in_hbm(array):
    return pltpu.with_memory_space_constraint(array, pltpu.HBM)


def params(**kwargs):
    return pltpu.CompilerParams(vmem_limit_bytes=VMEM_LIMIT, **kwargs)


def solution(mesh):
    rows_of_mesh = mesh.shape["ia"]
    columns_of_mesh = mesh.shape["ja"]

    def general(amplitudes, df_slabs, vir_irrep, occ_irrep, aux_irrep):
        occ_rows, pairs, vir_count, _ = amplitudes.shape
        count, window, _ = df_slabs.shape
        assert occ_rows == 1 and rows_of_mesh == pairs * columns_of_mesh
        pieces = 1
        while pieces * 2 <= min(rows_of_mesh, window // ROWS):
            pieces *= 2
        assert pieces * ROWS == window and rows_of_mesh % pieces == 0
        others = (columns_of_mesh - 1) * count

        own, piece = pl.pallas_call(
            functools.partial(piece_kernel, pieces),
            out_shape=(
                jax.ShapeDtypeStruct((count * window, vir_count), BF16),
                jax.ShapeDtypeStruct((count * ROWS, vir_count), BF16),
            ),
            in_specs=[hbm, smem, hbm],
            out_specs=(vmem, vmem),
            scratch_shapes=[
                pltpu.SMEM(vir_irrep.shape, jnp.int32),
                pltpu.VMEM((count, vir_count, window), BF16),
                pltpu.SemaphoreType.DMA((2,)),
            ],
            compiler_params=params(),
            name="mask_slab",
        )(in_hbm(vir_irrep), aux_irrep, in_hbm(jnp.transpose(df_slabs, (0, 2, 1))))
        got = [
            lax.ppermute(piece, "ja", [(j, j ^ s) for j in range(columns_of_mesh)])
            for s in range(columns_of_mesh - 1, 0, -1)
        ]
        tile, ladder = pl.pallas_call(
            own_kernel,
            out_shape=(
                pltpu.VMEM(amplitudes.shape, BF16),
                jax.ShapeDtypeStruct((pairs, window, window), F32),
            ),
            in_specs=[vmem, hbm],
            out_specs=(vmem, vmem),
            scratch_shapes=[pltpu.SemaphoreType.DMA((pairs,))],
            compiler_params=params(),
            cost_estimate=pl.CostEstimate(
                flops=2 * pairs * count * window * vir_count * vir_count,
                bytes_accessed=pairs * vir_count * vir_count * 2,
                transcendentals=0,
            ),
            name="own_slab",
        )(own, in_hbm(amplitudes))
        got, ladder = lax.optimization_barrier((got, ladder))
        joined = pl.pallas_call(
            join_kernel,
            out_shape=jax.ShapeDtypeStruct((others * ROWS, vir_count), BF16),
            in_specs=[vmem] * len(got),
            out_specs=vmem,
            compiler_params=params(),
            name="join_pieces",
        )(*got)
        held = {0: joined}
        for m in range(2, pieces, 2):
            held[m] = lax.ppermute(joined, "ia", [(i, i ^ m) for i in range(rows_of_mesh)])
        for m in range(0, pieces, 2):
            held[m + 1] = lax.ppermute(held[m], "ia", [(i, i ^ 1) for i in range(rows_of_mesh)])

        out = pl.pallas_call(
            functools.partial(rest_kernel, pieces, others),
            out_shape=(
                jax.ShapeDtypeStruct((pairs, window, window), F32),
                jax.ShapeDtypeStruct((pairs, window, window), BF16),
            ),
            in_specs=[smem, smem, vmem, vmem] + [vmem] * pieces,
            out_specs=(vmem, vmem),
            scratch_shapes=[pltpu.VMEM((others * window, vir_count), BF16)],
            compiler_params=params(),
            cost_estimate=pl.CostEstimate(
                flops=2 * pairs * others * window * vir_count * vir_count,
                bytes_accessed=others * window * vir_count * 2,
                transcendentals=0,
            ),
            name="other_slabs",
        )(vir_irrep, occ_irrep, ladder, pltpu.with_memory_space_constraint(tile, pltpu.VMEM), *[held[m] for m in range(pieces)])
        return tuple(out)

    def first_piece(df_slabs, vir_irrep, aux_irrep):
        count, window, vir_count = df_slabs.shape
        return pl.pallas_call(
            compact_kernel,
            out_shape=(
                jax.ShapeDtypeStruct((count, BLOCKS, TILE, 128), BF16),
                jax.ShapeDtypeStruct((1,), jnp.int32),
            ),
            in_specs=[hbm, smem, hbm],
            out_specs=(vmem, smem),
            scratch_shapes=[
                pltpu.SMEM(vir_irrep.shape, jnp.int32),
                pltpu.VMEM((count, vir_count, window), BF16),
                pltpu.VMEM((2, vir_count, window), BF16),
                pltpu.VMEM((window, WIDTH), BF16),
                pltpu.SemaphoreType.DMA((2,)),
            ],
            compiler_params=params(),
            name="compact_piece",
        )(in_hbm(vir_irrep), aux_irrep, in_hbm(jnp.transpose(df_slabs, (0, 2, 1))))

    def start_compact(piece, amplitudes, df_slabs, vir_irrep, occ_irrep, aux_irrep):
        _, pairs, vir_count, _ = amplitudes.shape
        count, window, _ = df_slabs.shape
        tiles = vir_irrep.shape[0]
        slab = in_hbm(jnp.transpose(df_slabs, (0, 2, 1)))
        mine = [
            lax.ppermute(piece, "ja", [(j, j ^ s) for j in range(columns_of_mesh)])
            for s in range(columns_of_mesh - 1, 0, -1)
        ]
        own, tile, stage = pl.pallas_call(
            sort_kernel,
            out_shape=(
                jax.ShapeDtypeStruct((count, BLOCKS, window, 128), BF16),
                pltpu.VMEM((2 * pairs, BLOCKS, WIDTH, 128), BF16),
                pltpu.VMEM((pairs, vir_count, vir_count), BF16),
            ),
            in_specs=[smem, smem, smem, pl.BlockSpec(memory_space=pl.ANY), hbm, hbm],
            out_specs=(vmem, vmem, vmem),
            scratch_shapes=[
                pltpu.VMEM((count, vir_count, window), BF16),
                pltpu.VMEM((2, vir_count, window), BF16),
                pltpu.SMEM((2, tiles), jnp.int32),
                pltpu.SemaphoreType.DMA,
                pltpu.SemaphoreType.DMA((pairs,)),
            ],
            compiler_params=params(),
            cost_estimate=pl.CostEstimate(
                flops=pairs * 2 * WIDTH * WIDTH * 8,
                bytes_accessed=pairs * vir_count * vir_count * 2,
                transcendentals=0,
            ),
            name="sort_amplitudes",
        )(vir_irrep, occ_irrep, aux_irrep, piece, slab, in_hbm(amplitudes))
        return mine, own, tile, stage

    def end_compact(mine, own, tile, stage, amplitudes, df_slabs, vir_irrep, occ_irrep, aux_irrep):
        _, pairs, _, _ = amplitudes.shape
        count, window, _ = df_slabs.shape
        total = count * columns_of_mesh
        rows = (total * window // BLOCK + 1) * BLOCK
        theirs = [lax.ppermute(p, "ia", [(i, i ^ 1) for i in range(rows_of_mesh)]) for p in mine]
        return pl.pallas_call(
            functools.partial(product_kernel, len(mine)),
            out_shape=(
                jax.ShapeDtypeStruct((pairs, window, window), F32),
                jax.ShapeDtypeStruct((pairs, window, window), BF16),
            ),
            in_specs=[smem, smem, smem, vmem, vmem, pl.BlockSpec(memory_space=pl.ANY)] + [vmem] * (2 * len(mine)),
            out_specs=(vmem, vmem),
            scratch_shapes=[
                pltpu.VMEM((rows, WIDTH), BF16),
                pltpu.VMEM((rows, WIDTH), BF16),
                pltpu.SMEM((total, 2), jnp.int32),
            ],
            compiler_params=params(),
            cost_estimate=pl.CostEstimate(
                flops=2 * pairs * total * window * WIDTH * WIDTH,
                bytes_accessed=total * window * WIDTH * 2,
                transcendentals=0,
            ),
            name="products",
        )(
            vir_irrep, occ_irrep, aux_irrep, own,
            pltpu.with_memory_space_constraint(tile, pltpu.VMEM),
            pltpu.with_memory_space_constraint(stage, pltpu.VMEM),
            *mine, *theirs,
        )

    def finish(ladder, sends):
        pairs = ladder.shape[0]

        def moves(step):
            return [
                (
                    i * columns_of_mesh + j,
                    (j * pairs + (i + step) % pairs) * columns_of_mesh + i // pairs,
                )
                for i in range(rows_of_mesh)
                for j in range(columns_of_mesh)
            ]

        if pairs != 2:
            return ladder, [
                lax.ppermute(sends[step : step + 1], ("ia", "ja"), moves(step)) for step in range(pairs)
            ]
        first = lax.ppermute(sends, ("ia", "ja"), moves(0))
        second = lax.ppermute(first, "ia", [(i, i ^ 1) for i in range(rows_of_mesh)])
        return ladder, [first, second]

    def add(ladder, received):
        pairs, window, _ = ladder.shape
        return pl.pallas_call(
            add_kernel,
            out_shape=jax.ShapeDtypeStruct((1, pairs, window, window), F32),
            in_specs=[vmem] * (pairs + 1),
            out_specs=vmem,
            compiler_params=params(),
            name="add_transposed",
        )(ladder, *received)

    def local(amplitudes, df_slabs, vir_irrep, occ_irrep, aux_irrep):
        window = df_slabs.shape[1]
        operands = (amplitudes, df_slabs, vir_irrep, occ_irrep, aux_irrep)
        if window != 2 * TILE or rows_of_mesh % 2:
            return add(*finish(*general(*operands)))
        piece, fits = first_piece(df_slabs, vir_irrep, aux_irrep)

        def compact():
            mine, own, tile, stage = start_compact(piece, *operands)
            mine, own = lax.optimization_barrier((mine, own))
            return add(*finish(*end_compact(mine, own, tile, stage, *operands)))

        return lax.cond(fits[0] == 1, compact, lambda: add(*finish(*general(*operands))))

    return jax.shard_map(
        local,
        mesh=mesh,
        in_specs=(P("ia", "ja", None, None), P("ja", None, None), P(), P(), P("ja")),
        out_specs=P("ia", "ja", None, None),
        check_vma=False,
    )
```

```python
import functools

import jax
import jax.numpy as jnp
from jax import lax
from jax.experimental import pallas as pl
from jax.experimental.pallas import tpu as pltpu
from jax.sharding import PartitionSpec as P

TILE = 64
ROWS = 16
SLOTS = 16
WIDTH = SLOTS * TILE
BLOCK = 256
BLOCKS = WIDTH // 128
GROUP = 4
F32 = jnp.float32
BF16 = jnp.bfloat16
VMEM_LIMIT = 32 * 1024 * 1024

smem = pl.BlockSpec(memory_space=pltpu.SMEM)
vmem = pl.BlockSpec(memory_space=pltpu.VMEM)
hbm = pl.BlockSpec(memory_space=pltpu.HBM)


def column_labels(vir_ref, tiles, columns):
    tile_of = lax.broadcasted_iota(jnp.int32, (1, columns), 1) // TILE
    labels = jnp.zeros((1, columns), jnp.int32)
    for tile in range(tiles):
        labels = jnp.where(tile_of == tile, vir_ref[tile], labels)
    return labels


def row_labels(vir_ref, first_row, rows, window):
    row = first_row + lax.broadcasted_iota(jnp.int32, (rows, 1), 0)
    labels = jnp.zeros((rows, 1), jnp.int32)
    for tile in range(window // TILE):
        labels = jnp.where(row // TILE == tile, vir_ref[tile], labels)
    return labels


def masked(block, rows_label, columns_label, aux):
    return jnp.where((rows_label ^ columns_label) == aux, block, jnp.zeros_like(block))


def piece_kernel(pieces, vir_hbm, aux_ref, slab_hbm, own_ref, piece_ref, vir_ref, slab_ref, sem):
    copies = [
        pltpu.make_async_copy(slab_hbm, slab_ref, sem.at[0]),
        pltpu.make_async_copy(vir_hbm, vir_ref, sem.at[1]),
    ]
    for copy in copies:
        copy.start()
    for copy in copies:
        copy.wait()
    count, columns, window = slab_ref.shape
    first = pl.multiple_of(lax.rem(lax.axis_index("ia"), pieces) * ROWS, ROWS)
    labels = column_labels(vir_ref, vir_ref.shape[0], columns)
    rows = row_labels(vir_ref, 0, window, window)
    for aux in range(count):
        own_ref[aux * window : (aux + 1) * window, :] = masked(slab_ref[aux].T, rows, labels, aux_ref[aux])
        piece_ref[aux * ROWS : (aux + 1) * ROWS, :] = own_ref[pl.ds(aux * window + first, ROWS), :]


def join_kernel(*refs):
    out_ref = refs[-1]
    at = 0
    for ref in refs[:-1]:
        out_ref[at : at + ref.shape[0], :] = ref[...]
        at += ref.shape[0]


def chunks(columns):
    step = 512
    starts = list(range(0, columns, step))
    if len(starts) > 1 and columns - starts[-1] < 128:
        starts.pop()
    return list(zip(starts, starts[1:] + [columns]))


def add_ladder(tile_ref, pair, slabs, ladder):
    columns = slabs.shape[1]
    window = ladder.shape[0]
    for lo, hi in chunks(columns):
        half = jnp.dot(slabs[...], tile_ref[0, pair, :, lo:hi], preferred_element_type=F32).astype(BF16)
        for start in range(0, slabs.shape[0], window):
            ladder = ladder + lax.dot_general(
                half[start : start + window],
                slabs[start : start + window, lo:hi],
                (((1,), (1,)), ((), ())),
                preferred_element_type=F32,
            )
    return ladder


def own_kernel(own_ref, t_ref, tile_ref, ladder_ref, sem):
    window = ladder_ref.shape[1]
    copies = []
    for pair in range(t_ref.shape[1]):
        copies.append(pltpu.make_async_copy(t_ref.at[0, pair], tile_ref.at[0, pair], sem.at[pair]))
        copies[-1].start()
    for pair in range(t_ref.shape[1]):
        copies[pair].wait()
        ladder_ref[pair] = add_ladder(tile_ref, pair, own_ref, jnp.zeros((window, window), F32))


def rest_kernel(pieces, others, vir_ref, occ_ref, ladder_ref, tile_ref, *refs):
    piece_refs = refs[:pieces]
    out_ref = refs[pieces]
    pairs = tile_ref.shape[1]
    send_ref = refs[pieces + 1]
    slabs = refs[-1]
    window = out_ref.shape[1]
    row = lax.axis_index("ia")
    column = lax.axis_index("ja") * pairs
    mine = lax.rem(row, pieces)
    for m in range(pieces):
        first = pl.multiple_of((mine ^ m) * ROWS, ROWS)
        for slab in range(others):
            slabs[pl.ds(slab * window + first, ROWS), :] = piece_refs[m][slab * ROWS : (slab + 1) * ROWS, :]
    left = row_labels(vir_ref, 0, window, window)
    right = column_labels(vir_ref, window // TILE, window)
    for pair in range(pairs):
        ladder = add_ladder(tile_ref, pair, slabs, ladder_ref[pair])
        keep = (left ^ right) == (occ_ref[row] ^ occ_ref[column + pair])
        out_ref[pair] = jnp.where(keep, ladder, jnp.zeros_like(ladder))
    for step in range(pairs):
        block = out_ref[lax.rem(row + step, pairs)]
        send_ref[step] = block.T.astype(BF16)


def places_of(vir_ref):
    places = []
    ones = jnp.int32(0)
    for tile in range(vir_ref.shape[0]):
        label = vir_ref[tile]
        places.append((label, jnp.where(label == 1, ones, tile - ones)))
        ones = ones + label
    return places, (vir_ref.shape[0] - ones, ones)


def tile_rows(place):
    return pl.ds(pl.multiple_of(place * TILE, TILE), TILE)


def compact_rows(slab, places, numbers, label, sorted_ref):
    tiles = len(places)
    for tile, (of, place) in enumerate(places):
        sorted_ref[of, tile_rows(place), :] = slab[tile * TILE : (tile + 1) * TILE, :]
    number = jnp.where(label == 1, numbers[1], numbers[0])
    block = sorted_ref[label, :WIDTH, :].T
    column = lax.broadcasted_iota(jnp.int32, (16, WIDTH), 1)
    mark = jnp.where((column == WIDTH - 1) & (number * 2 < tiles), 1.0, 0.0).astype(BF16)
    keep = column < number * TILE
    rows = block.shape[0]
    return jnp.concatenate(
        [jnp.where(keep, block[r : r + 16], mark) for r in range(0, rows, 16)], axis=0
    )


def compact_kernel(vir_hbm, aux_ref, slab_hbm, piece_ref, fits_ref, vir_ref, slab_ref, sorted_ref, turned_ref, sem):
    copies = [
        pltpu.make_async_copy(slab_hbm, slab_ref, sem.at[0]),
        pltpu.make_async_copy(vir_hbm, vir_ref, sem.at[1]),
    ]
    for copy in copies:
        copy.start()
    copies[1].wait()
    places, numbers = places_of(vir_ref)
    fits_ref[0] = jnp.where(jnp.maximum(numbers[0], numbers[1]) <= SLOTS, 1, 0)
    core = lax.rem(lax.axis_index("ia"), 2)
    copies[0].wait()
    for aux in range(slab_ref.shape[0]):
        label = aux_ref[aux] ^ vir_ref[core]
        turned_ref[...] = compact_rows(slab_ref[aux], places, numbers, label, sorted_ref)
        for q in range(BLOCKS):
            piece_ref[aux, q] = turned_ref[tile_rows(core), q * 128 : (q + 1) * 128]


def sort_kernel(
    vir_ref, occ_ref, aux_ref, after_ref, slab_hbm, t_hbm, own_ref, out_ref, stage_ref,
    slab_ref, rows_ref, lists_ref, slab_sem, sem,
):
    del after_ref
    pairs = t_hbm.shape[1]
    columns = t_hbm.shape[3]
    tiles = vir_ref.shape[0]
    row = lax.axis_index("ia")
    column = lax.axis_index("ja") * pairs
    full = columns // 128
    moves = [pltpu.make_async_copy(t_hbm.at[0, pair], stage_ref.at[pair], sem.at[pair]) for pair in range(pairs)]
    for move in moves:
        move.start()
    own_copy = pltpu.make_async_copy(slab_hbm, slab_ref, slab_sem)
    own_copy.start()
    places, numbers = places_of(vir_ref)
    for label in range(2):
        for place in range(SLOTS):
            lists_ref[label, place] = -1
    for tile, (label, place) in enumerate(places):
        lists_ref[label, place] = tile
    own_copy.wait()
    count, _, window = slab_ref.shape
    for aux in range(count):
        for chunk in range(2):
            label = aux_ref[aux] ^ vir_ref[chunk]
            block = compact_rows(slab_ref[aux], places, numbers, label, rows_ref)
            for q in range(BLOCKS):
                own_ref[aux, q, chunk * TILE : (chunk + 1) * TILE, :] = block[
                    chunk * TILE : (chunk + 1) * TILE, q * 128 : (q + 1) * 128
                ]
    sort_units(
        [(0, 1)] * (pairs - 1) + [(0,)], lambda pair: moves[pair].wait(),
        vir_ref, occ_ref, stage_ref, lists_ref, numbers, out_ref,
    )


def last_kernel(vir_ref, occ_ref, after_ref, stage_ref, tile_ref, out_ref, lists_ref):
    del after_ref, tile_ref
    places, numbers = places_of(vir_ref)
    for label in range(2):
        for place in range(SLOTS):
            lists_ref[label, place] = -1
    for tile, (label, place) in enumerate(places):
        lists_ref[label, place] = tile
    pairs = stage_ref.shape[0]
    sort_units(
        [()] * (pairs - 1) + [(1,)], lambda pair: None,
        vir_ref, occ_ref, stage_ref, lists_ref, numbers, out_ref,
    )


def sort_units(chosen, ready, vir_ref, occ_ref, stage_ref, lists_ref, numbers, out_ref):
    pairs, _, columns = stage_ref.shape
    tiles = vir_ref.shape[0]
    row = lax.axis_index("ia")
    column = lax.axis_index("ja") * pairs
    full = columns // 128
    lower = lax.broadcasted_iota(jnp.int32, (TILE, 128), 1) < TILE
    for pair in range(pairs):
        if not chosen[pair]:
            continue
        ready(pair)
        symbol = occ_ref[row] ^ occ_ref[column + pair]

        for label in chosen[pair]:
            rows_of = jnp.where(label == 1, numbers[1], numbers[0])
            columns_of = jnp.where((label ^ symbol) == 1, numbers[1], numbers[0])

            def block(q, carry, label=label, rows_of=rows_of):
                known = [
                    jnp.clip(lists_ref[label ^ symbol, 2 * q + upper], 0, 2 * full - 1) for upper in range(2)
                ]
                spots = [pl.ds(pl.multiple_of((k // 2) * 128, 128), 128) for k in known]
                sides = [lax.rem(k, 2) for k in known]

                def move(left, right, number):
                    for group in range(0, number, GROUP):
                        joined = []
                        for place in range(group, group + GROUP):
                            rows = tile_rows(jnp.maximum(lists_ref[label, place], 0))
                            low, high = [stage_ref[pair, rows, spot] for spot in spots]
                            if left and not right:
                                value = pltpu.roll(jnp.where(lower, high, low), TILE, 1)
                            else:
                                value = jnp.where(
                                    lower,
                                    pltpu.roll(low, TILE, 1) if left else low,
                                    high if right else pltpu.roll(high, TILE, 1),
                                )
                            joined.append(value)
                        out_ref[2 * pair + label, q, group * TILE : (group + GROUP) * TILE, :] = (
                            jnp.concatenate(joined, axis=0)
                        )

                for left in range(2):
                    for right in range(2):
                        here = (sides[0] == left) & (sides[1] == right)
                        few = rows_of <= SLOTS - GROUP
                        pl.when(here & few)(functools.partial(move, left, right, SLOTS - GROUP))
                        pl.when(here & jnp.logical_not(few))(functools.partial(move, left, right, SLOTS))
                return carry

            lax.fori_loop(0, jnp.minimum((columns_of + 1) // 2, BLOCKS), block, 0)
        empty = jnp.zeros((TILE, TILE), BF16)
        if columns % 128:
            last = vir_ref[tiles - 1]
            end = jnp.where(last == 1, numbers[1], numbers[0]) - 1
            label = last ^ symbol
            q = jnp.minimum(end // 2, BLOCKS - 1)
            here = label == chosen[pair][0] if len(chosen[pair]) == 1 else label >= 0
            for upper in range(2):

                @pl.when((lax.rem(end, 2) == upper) & (end < SLOTS) & here)
                def _(upper=upper):
                    for place in range(SLOTS):
                        rows = tile_rows(jnp.maximum(lists_ref[label, place], 0))
                        value = stage_ref[pair, rows, full * 128 :]
                        at = (2 * pair + label, q, slice(place * TILE, (place + 1) * TILE), slice(None))
                        both = [value, empty] if upper == 0 else [out_ref[at][:, :TILE], value]
                        out_ref[at] = jnp.concatenate(both, axis=1)

        for label in chosen[pair]:
            number = jnp.where((label ^ symbol) == 1, numbers[1], numbers[0])

            def clear_block(q, carry):
                out_ref[2 * pair + label, q] = jnp.zeros((WIDTH, 128), BF16)
                return carry

            lax.fori_loop((number + 1) // 2, BLOCKS, clear_block, 0)

            @pl.when((lax.rem(number, 2) == 1) & (number < SLOTS))
            def _():
                q = number // 2
                for place in range(SLOTS):
                    rows = slice(place * TILE, (place + 1) * TILE)
                    value = out_ref[2 * pair + label, q, rows, :]
                    out_ref[2 * pair + label, q, rows, :] = jnp.concatenate([value[:, :TILE], empty], axis=1)

        for label in chosen[pair]:

            def clear(place, carry):
                for q in range(BLOCKS):
                    out_ref[2 * pair + label, q, tile_rows(place), :] = jnp.zeros((TILE, 128), BF16)
                return carry

            lax.fori_loop(numbers[label], SLOTS, clear, 0)


def product_kernel(arrived, vir_ref, occ_ref, aux_ref, own_ref, sorted_ref, stage_ref, *refs):
    del stage_ref
    mine_refs, their_refs = refs[:arrived], refs[arrived : 2 * arrived]
    out_ref = refs[2 * arrived]
    pairs, window, _ = out_ref.shape
    send_ref = refs[2 * arrived + 1]
    slabs_ref, half_ref, place_ref = refs[-3:]
    count = own_ref.shape[0]
    total = count * (arrived + 1)
    tiles = vir_ref.shape[0]
    row = lax.axis_index("ia")
    column = lax.axis_index("ja") * pairs
    core = lax.rem(row, 2)
    ones = jnp.int32(0)
    for tile in range(tiles):
        ones = ones + vir_ref[tile]
    smaller = jnp.where(ones * 2 < tiles, 1, 0)

    auxes = [aux_ref[aux] for aux in range(count)]
    for ref in mine_refs:
        for aux in range(count):
            mark = ref[aux, BLOCKS - 1, :16, :].astype(F32)
            marked = jnp.max(mark) > 0.5
            label = jnp.where(marked, smaller, 1 - smaller)
            auxes.append(label ^ vir_ref[core])
    places = [[jnp.int32(0)] * 2 for _ in range(total)]
    rows_of = [jnp.int32(0), jnp.int32(0)]
    labels = [[aux ^ vir_ref[chunk] for chunk in range(2)] for aux in auxes]
    for slab in range(total):
        for chunk in range(2):
            label = labels[slab][chunk]
            places[slab][chunk] = jnp.where(label == 1, rows_of[1], rows_of[0])
            rows_of = [rows_of[0] + (1 - label) * TILE, rows_of[1] + label * TILE]
    first_blocks = (rows_of[0] + (BLOCK - 1)) // BLOCK
    blocks = first_blocks + (rows_of[1] + (BLOCK - 1)) // BLOCK
    for slab in range(total):
        for chunk in range(2):
            place_ref[slab, chunk] = places[slab][chunk] + labels[slab][chunk] * first_blocks * BLOCK

    def at(slab, chunk):
        return pl.ds(pl.multiple_of(place_ref[slab, chunk], TILE), TILE)

    for aux in range(count):
        for chunk in range(2):
            for q in range(BLOCKS):
                slabs_ref[at(aux, chunk), q * 128 : (q + 1) * 128] = own_ref[
                    aux, q, chunk * TILE : (chunk + 1) * TILE, :
                ]
    for m in range(arrived):
        for aux in range(count):
            slab = (m + 1) * count + aux
            for q in range(BLOCKS):
                slabs_ref[at(slab, core), q * 128 : (q + 1) * 128] = mine_refs[m][aux, q]
                slabs_ref[at(slab, 1 - core), q * 128 : (q + 1) * 128] = their_refs[m][aux, q]

    left = row_labels(vir_ref, 0, window, window)
    right = column_labels(vir_ref, window // TILE, window)

    def one_pair(pair, carry):
        symbol = occ_ref[row] ^ occ_ref[column + pair]
        out_ref[pair] = jnp.zeros((window, window), F32)

        @pl.when((vir_ref[0] != vir_ref[1]) | (symbol == 0))
        def _():
            def first(block, inner):
                label = jnp.where(block < first_blocks, 0, 1)
                rows = pl.ds(pl.multiple_of(block * BLOCK, BLOCK), BLOCK)
                for lo in range(0, WIDTH, 512):
                    half_ref[rows, lo : lo + 512] = jnp.dot(
                        slabs_ref[rows, :],
                        jnp.concatenate(
                            [sorted_ref[2 * pair + label, (lo + at) // 128] for at in range(0, 512, 128)], axis=1
                        ),
                        preferred_element_type=F32,
                    ).astype(BF16)
                return inner

            lax.fori_loop(0, blocks, first, 0)
            ladder = jnp.zeros((window, window), F32)
            for slab in range(total):
                halves = jnp.concatenate([half_ref[at(slab, 0), :], half_ref[at(slab, 1), :]], axis=0)
                others = jnp.concatenate([slabs_ref[at(slab, 0), :], slabs_ref[at(slab, 1), :]], axis=0)
                ladder = ladder + lax.dot_general(
                    halves, others, (((1,), (1,)), ((), ())), preferred_element_type=F32
                )
            out_ref[pair] = jnp.where((left ^ right) == symbol, ladder, jnp.zeros_like(ladder))

        return carry

    lax.fori_loop(0, pairs, one_pair, 0)
    for step in range(pairs):
        block = out_ref[lax.rem(row + step, pairs)]
        send_ref[step] = block.T.astype(BF16)


def add_kernel(ladder_ref, *refs):
    out_ref = refs[-1]
    pairs = ladder_ref.shape[0]
    row = lax.axis_index("ia")
    for step in range(pairs):
        slot = lax.rem(row + (pairs - step), pairs)
        block = refs[step][min(step, refs[step].shape[0] - 1)]
        out_ref[0, slot] = ladder_ref[slot] + block.astype(F32)


def in_hbm(array):
    return pltpu.with_memory_space_constraint(array, pltpu.HBM)


def params(**kwargs):
    return pltpu.CompilerParams(vmem_limit_bytes=VMEM_LIMIT, **kwargs)


def solution(mesh):
    rows_of_mesh = mesh.shape["ia"]
    columns_of_mesh = mesh.shape["ja"]

    def general(amplitudes, df_slabs, vir_irrep, occ_irrep, aux_irrep):
        occ_rows, pairs, vir_count, _ = amplitudes.shape
        count, window, _ = df_slabs.shape
        assert occ_rows == 1 and rows_of_mesh == pairs * columns_of_mesh
        pieces = 1
        while pieces * 2 <= min(rows_of_mesh, window // ROWS):
            pieces *= 2
        assert pieces * ROWS == window and rows_of_mesh % pieces == 0
        others = (columns_of_mesh - 1) * count

        own, piece = pl.pallas_call(
            functools.partial(piece_kernel, pieces),
            out_shape=(
                jax.ShapeDtypeStruct((count * window, vir_count), BF16),
                jax.ShapeDtypeStruct((count * ROWS, vir_count), BF16),
            ),
            in_specs=[hbm, smem, hbm],
            out_specs=(vmem, vmem),
            scratch_shapes=[
                pltpu.SMEM(vir_irrep.shape, jnp.int32),
                pltpu.VMEM((count, vir_count, window), BF16),
                pltpu.SemaphoreType.DMA((2,)),
            ],
            compiler_params=params(),
            name="mask_slab",
        )(in_hbm(vir_irrep), aux_irrep, in_hbm(jnp.transpose(df_slabs, (0, 2, 1))))
        got = [
            lax.ppermute(piece, "ja", [(j, j ^ s) for j in range(columns_of_mesh)])
            for s in range(columns_of_mesh - 1, 0, -1)
        ]
        tile, ladder = pl.pallas_call(
            own_kernel,
            out_shape=(
                pltpu.VMEM(amplitudes.shape, BF16),
                jax.ShapeDtypeStruct((pairs, window, window), F32),
            ),
            in_specs=[vmem, hbm],
            out_specs=(vmem, vmem),
            scratch_shapes=[pltpu.SemaphoreType.DMA((pairs,))],
            compiler_params=params(),
            cost_estimate=pl.CostEstimate(
                flops=2 * pairs * count * window * vir_count * vir_count,
                bytes_accessed=pairs * vir_count * vir_count * 2,
                transcendentals=0,
            ),
            name="own_slab",
        )(own, in_hbm(amplitudes))
        got, ladder = lax.optimization_barrier((got, ladder))
        joined = pl.pallas_call(
            join_kernel,
            out_shape=jax.ShapeDtypeStruct((others * ROWS, vir_count), BF16),
            in_specs=[vmem] * len(got),
            out_specs=vmem,
            compiler_params=params(),
            name="join_pieces",
        )(*got)
        held = {0: joined}
        for m in range(2, pieces, 2):
            held[m] = lax.ppermute(joined, "ia", [(i, i ^ m) for i in range(rows_of_mesh)])
        for m in range(0, pieces, 2):
            held[m + 1] = lax.ppermute(held[m], "ia", [(i, i ^ 1) for i in range(rows_of_mesh)])

        out = pl.pallas_call(
            functools.partial(rest_kernel, pieces, others),
            out_shape=(
                jax.ShapeDtypeStruct((pairs, window, window), F32),
                jax.ShapeDtypeStruct((pairs, window, window), BF16),
            ),
            in_specs=[smem, smem, vmem, vmem] + [vmem] * pieces,
            out_specs=(vmem, vmem),
            scratch_shapes=[pltpu.VMEM((others * window, vir_count), BF16)],
            compiler_params=params(),
            cost_estimate=pl.CostEstimate(
                flops=2 * pairs * others * window * vir_count * vir_count,
                bytes_accessed=others * window * vir_count * 2,
                transcendentals=0,
            ),
            name="other_slabs",
        )(vir_irrep, occ_irrep, ladder, pltpu.with_memory_space_constraint(tile, pltpu.VMEM), *[held[m] for m in range(pieces)])
        return tuple(out)

    def first_piece(df_slabs, vir_irrep, aux_irrep):
        count, window, vir_count = df_slabs.shape
        return pl.pallas_call(
            compact_kernel,
            out_shape=(
                jax.ShapeDtypeStruct((count, BLOCKS, TILE, 128), BF16),
                jax.ShapeDtypeStruct((1,), jnp.int32),
            ),
            in_specs=[hbm, smem, hbm],
            out_specs=(vmem, smem),
            scratch_shapes=[
                pltpu.SMEM(vir_irrep.shape, jnp.int32),
                pltpu.VMEM((count, vir_count, window), BF16),
                pltpu.VMEM((2, vir_count, window), BF16),
                pltpu.VMEM((window, WIDTH), BF16),
                pltpu.SemaphoreType.DMA((2,)),
            ],
            compiler_params=params(),
            name="compact_piece",
        )(in_hbm(vir_irrep), aux_irrep, in_hbm(jnp.transpose(df_slabs, (0, 2, 1))))

    def start_compact(piece, amplitudes, df_slabs, vir_irrep, occ_irrep, aux_irrep):
        _, pairs, vir_count, _ = amplitudes.shape
        count, window, _ = df_slabs.shape
        tiles = vir_irrep.shape[0]
        slab = in_hbm(jnp.transpose(df_slabs, (0, 2, 1)))
        mine = [
            lax.ppermute(piece, "ja", [(j, j ^ s) for j in range(columns_of_mesh)])
            for s in range(columns_of_mesh - 1, 0, -1)
        ]
        own, tile, stage = pl.pallas_call(
            sort_kernel,
            out_shape=(
                jax.ShapeDtypeStruct((count, BLOCKS, window, 128), BF16),
                pltpu.VMEM((2 * pairs, BLOCKS, WIDTH, 128), BF16),
                pltpu.VMEM((pairs, vir_count, vir_count), BF16),
            ),
            in_specs=[smem, smem, smem, pl.BlockSpec(memory_space=pl.ANY), hbm, hbm],
            out_specs=(vmem, vmem, vmem),
            scratch_shapes=[
                pltpu.VMEM((count, vir_count, window), BF16),
                pltpu.VMEM((2, vir_count, window), BF16),
                pltpu.SMEM((2, tiles), jnp.int32),
                pltpu.SemaphoreType.DMA,
                pltpu.SemaphoreType.DMA((pairs,)),
            ],
            compiler_params=params(),
            cost_estimate=pl.CostEstimate(
                flops=pairs * 2 * WIDTH * WIDTH * 8,
                bytes_accessed=pairs * vir_count * vir_count * 2,
                transcendentals=0,
            ),
            name="sort_amplitudes",
        )(vir_irrep, occ_irrep, aux_irrep, piece, slab, in_hbm(amplitudes))
        return mine, own, tile, stage

    def end_compact(mine, own, tile, stage, amplitudes, df_slabs, vir_irrep, occ_irrep, aux_irrep):
        _, pairs, _, _ = amplitudes.shape
        count, window, _ = df_slabs.shape
        total = count * columns_of_mesh
        rows = (total * window // BLOCK + 1) * BLOCK
        theirs = [lax.ppermute(p, "ia", [(i, i ^ 1) for i in range(rows_of_mesh)]) for p in mine]
        tile = pl.pallas_call(
            last_kernel,
            out_shape=pltpu.VMEM(tile.shape, BF16),
            in_specs=[smem, smem, pl.BlockSpec(memory_space=pl.ANY), vmem, pl.BlockSpec(memory_space=pl.ANY)],
            out_specs=vmem,
            input_output_aliases={4: 0},
            scratch_shapes=[pltpu.SMEM((2, vir_irrep.shape[0]), jnp.int32)],
            compiler_params=params(),
            name="sort_last",
        )(
            vir_irrep, occ_irrep, mine[-1],
            pltpu.with_memory_space_constraint(stage, pltpu.VMEM),
            pltpu.with_memory_space_constraint(tile, pltpu.VMEM),
        )
        theirs, own, tile = lax.optimization_barrier((theirs, own, tile))
        return pl.pallas_call(
            functools.partial(product_kernel, len(mine)),
            out_shape=(
                jax.ShapeDtypeStruct((pairs, window, window), F32),
                jax.ShapeDtypeStruct((pairs, window, window), BF16),
            ),
            in_specs=[smem, smem, smem, vmem, vmem, pl.BlockSpec(memory_space=pl.ANY)] + [vmem] * (2 * len(mine)),
            out_specs=(vmem, vmem),
            scratch_shapes=[
                pltpu.VMEM((rows, WIDTH), BF16),
                pltpu.VMEM((rows, WIDTH), BF16),
                pltpu.SMEM((total, 2), jnp.int32),
            ],
            compiler_params=params(),
            cost_estimate=pl.CostEstimate(
                flops=2 * pairs * total * window * WIDTH * WIDTH,
                bytes_accessed=total * window * WIDTH * 2,
                transcendentals=0,
            ),
            name="products",
        )(
            vir_irrep, occ_irrep, aux_irrep, own,
            pltpu.with_memory_space_constraint(tile, pltpu.VMEM),
            pltpu.with_memory_space_constraint(stage, pltpu.VMEM),
            *mine, *theirs,
        )

    def finish(ladder, sends):
        pairs = ladder.shape[0]

        def moves(step):
            return [
                (
                    i * columns_of_mesh + j,
                    (j * pairs + (i + step) % pairs) * columns_of_mesh + i // pairs,
                )
                for i in range(rows_of_mesh)
                for j in range(columns_of_mesh)
            ]

        if pairs != 2:
            return ladder, [
                lax.ppermute(sends[step : step + 1], ("ia", "ja"), moves(step)) for step in range(pairs)
            ]
        first = lax.ppermute(sends, ("ia", "ja"), moves(0))
        second = lax.ppermute(first, "ia", [(i, i ^ 1) for i in range(rows_of_mesh)])
        return ladder, [first, second]

    def add(ladder, received):
        pairs, window, _ = ladder.shape
        return pl.pallas_call(
            add_kernel,
            out_shape=jax.ShapeDtypeStruct((1, pairs, window, window), F32),
            in_specs=[vmem] * (pairs + 1),
            out_specs=vmem,
            compiler_params=params(),
            name="add_transposed",
        )(ladder, *received)

    def local(amplitudes, df_slabs, vir_irrep, occ_irrep, aux_irrep):
        window = df_slabs.shape[1]
        operands = (amplitudes, df_slabs, vir_irrep, occ_irrep, aux_irrep)
        if window != 2 * TILE or rows_of_mesh % 2:
            return add(*finish(*general(*operands)))
        piece, fits = first_piece(df_slabs, vir_irrep, aux_irrep)

        def compact():
            mine, own, tile, stage = start_compact(piece, *operands)
            mine, own = lax.optimization_barrier((mine, own))
            return add(*finish(*end_compact(mine, own, tile, stage, *operands)))

        return lax.cond(fits[0] == 1, compact, lambda: add(*finish(*general(*operands))))

    return jax.shard_map(
        local,
        mesh=mesh,
        in_specs=(P("ia", "ja", None, None), P("ja", None, None), P(), P(), P("ja")),
        out_specs=P("ia", "ja", None, None),
        check_vma=False,
    )
```
